128 devices in a mesh: blk: 16 (over z_hi, x, core), uly: 8 (over y, z_lo).
Axes of the slice: x: 4, y: 4, z: 4 (z_hi: 2, z_lo: 2; z = z_hi * 2 + z_lo), core: 2. Of those that a mesh axis runs over, the one named last changes fastest.
Arguments:
- queries: bfloat16 [16384, 4096], P(('blk', 'uly')), may hold values from -6 to 6
- input_keys: bfloat16 [16384, 1024], P(('blk', 'uly')), may hold values from -6 to 6
- input_values: bfloat16 [16384, 1024], P(('blk', 'uly')), may hold values from -6 to 6
- outputs: bfloat16 [16384, 4096], P(('blk', 'uly')), may hold values from -2 to 2
- output_gradient: bfloat16 [16384, 4096], P(('blk', 'uly')), may hold values from -6 to 6
- saved_logsumexp: float32 [16384, 32], P(('blk', 'uly')), may hold values from -0.5 to 12
- span_order: int32 [16, 2], replicated, may hold values from 0 to 31, as said below
Outputs:
- grad_queries: bfloat16 [16384, 4096], P(('blk', 'uly'))
- key_gradient: bfloat16 [16384, 1024], P(('blk', 'uly'))
- value_gradient: bfloat16 [16384, 1024], P(('blk', 'uly'))
The draws below stay inside these ranges and needn't reach their ends.
Inputs may be any that keep to these rules, and one draw needn't show every extreme that they name: `span_order`: row r names two position blocks c and 31 - c for some c, in either order; every block of 0 to 31 appears exactly once in the table.
All inputs are finite; a program needn't handle non-finite values.
Results may differ from the reference program's by a relative error of at most 0.005.
Values may be sent and summed in bfloat16 or wider, within the bound.
No kernel may reach another device: no remote copies, remote signals or barrier semaphores. Data moves between devices by JAX's collectives and lax.ppermute only.
A program may use at most 128 MiB of HBM per device.

```python
import math
import jax
import jax.numpy as jnp
from jax import lax

QUERY_HEADS = 32
KEY_VALUE_HEADS = 8
HEAD_DIMENSION = 128
SEQUENCE_LENGTH = 16384
SPAN = 512
SLOT = 1024
N_BLK = 16


def mirror_pairs(key):
    order = jax.random.permutation(key, N_BLK).astype(jnp.int32)
    flips = jax.random.randint(jax.random.fold_in(key, 7), (N_BLK,), 0, 2)
    mirror = 2 * N_BLK - 1 - order
    first = jnp.where(flips == 1, mirror, order)
    second = jnp.where(flips == 1, order, mirror)
    return jnp.stack([first, second], axis=1).astype(jnp.int32)


def draw_span_order(key, part):
    return mirror_pairs(key)


def draw_saved_logsumexp(key, part):
    key = jax.random.fold_in(key, 3)
    base = jnp.log(jnp.full((SEQUENCE_LENGTH, 1), SLOT, jnp.float32))
    noise = jax.random.uniform(key, (SEQUENCE_LENGTH, QUERY_HEADS), jnp.float32, 0.1, 0.9)
    return base + noise


def level_of(key, dims, shards, low, high):
    gain, own = 1.0, jax.random.fold_in(key, 6)
    for dim, parts in shards:
        steps = jnp.exp(jax.random.uniform(jax.random.fold_in(own, dim), (parts,), jnp.float32, low / len(shards), high / len(shards)))
        gain = gain * jnp.repeat(steps, dims[dim] // parts).reshape([-1 if axis == dim else 1 for axis in range(len(dims))])
    return gain


def normal_values(stream_key, extent, width, bound, cuts=(), kind=jnp.bfloat16):
    entries = jax.random.normal(stream_key, extent, jnp.float32) * width
    if len(cuts) > 0:
        entries = level_of(stream_key, extent, cuts, -0.22, 0.18) * entries
    return jnp.clip(entries, min=-bound, max=bound).astype(kind)


def setup_inputs(seed: int = 0) -> dict:
    key_of = jax.random.split(jax.random.key(seed), 8)
    queries = normal_values(key_of[0], (SEQUENCE_LENGTH, QUERY_HEADS * HEAD_DIMENSION), 1.0, 6.0, ((0, 128),))
    input_keys = normal_values(key_of[1], (SEQUENCE_LENGTH, KEY_VALUE_HEADS * HEAD_DIMENSION), 1.0, 6.0, ((0, 128),))
    input_values = normal_values(key_of[2], (SEQUENCE_LENGTH, KEY_VALUE_HEADS * HEAD_DIMENSION), 1.0, 6.0, ((0, 128),))
    outputs = normal_values(key_of[3], (SEQUENCE_LENGTH, QUERY_HEADS * HEAD_DIMENSION), 0.3, 2.0, ((0, 128),))
    output_gradient = normal_values(key_of[4], (SEQUENCE_LENGTH, QUERY_HEADS * HEAD_DIMENSION), 1.0, 6.0, ((0, 128),))
    saved_logsumexp = draw_saved_logsumexp(jax.random.fold_in(key_of[7], 71), 0)
    span_order = draw_span_order(jax.random.fold_in(key_of[7], 71), 0)
    return dict(queries=queries, input_keys=input_keys, input_values=input_values, outputs=outputs, output_gradient=output_gradient, saved_logsumexp=saved_logsumexp, span_order=span_order)


def reference(queries, input_keys, input_values, outputs, output_gradient, saved_logsumexp, span_order):
    row_ids = jnp.arange(SEQUENCE_LENGTH, dtype=jnp.int32)
    blocks = span_order[row_ids // (2 * SPAN), row_ids // SPAN % 2]
    positions = (blocks * SPAN + row_ids % SPAN).astype(jnp.int32)
    query_groups = QUERY_HEADS // KEY_VALUE_HEADS
    factor = 1.0 / math.sqrt(HEAD_DIMENSION)
    row_delta_values = (output_gradient.astype(jnp.float32) * outputs.astype(jnp.float32)).reshape(SEQUENCE_LENGTH, QUERY_HEADS, HEAD_DIMENSION).sum(axis=2)
    query_per_head = queries.reshape(SEQUENCE_LENGTH, KEY_VALUE_HEADS, query_groups, HEAD_DIMENSION).transpose(1, 0, 2, 3)
    gradient_per_head = output_gradient.reshape(SEQUENCE_LENGTH, KEY_VALUE_HEADS, query_groups, HEAD_DIMENSION).transpose(1, 0, 2, 3)
    key_per_head = input_keys.reshape(SEQUENCE_LENGTH, KEY_VALUE_HEADS, HEAD_DIMENSION).transpose(1, 0, 2)
    value_per_head = input_values.reshape(SEQUENCE_LENGTH, KEY_VALUE_HEADS, HEAD_DIMENSION).transpose(1, 0, 2)
    logsumexp_per_head = saved_logsumexp.reshape(SEQUENCE_LENGTH, KEY_VALUE_HEADS, query_groups).transpose(1, 0, 2)
    delta_per_head = row_delta_values.reshape(SEQUENCE_LENGTH, KEY_VALUE_HEADS, query_groups).transpose(1, 0, 2)

    def per_head(head_inputs):
        query_one, grad_one, key_one, value_one, sums_one, delta_one = head_inputs
        key_wide = key_one.astype(jnp.float32)
        value_wide = value_one.astype(jnp.float32)

        def slot_step(state_pair, slot_index):
            key_gradient, value_gradient = state_pair
            start = (slot_index * SLOT).astype(jnp.int32)
            prev = ((slot_index + N_BLK - 1) % N_BLK * SLOT).astype(jnp.int32)
            query_blk = lax.dynamic_slice_in_dim(query_one, start, SLOT, 0).astype(jnp.float32)
            grad_blk = lax.dynamic_slice_in_dim(grad_one, start, SLOT, 0).astype(jnp.float32)
            sums_blk = lax.dynamic_slice_in_dim(sums_one, start, SLOT, 0)
            delta_blk = lax.dynamic_slice_in_dim(delta_one, start, SLOT, 0)
            pos_blk = lax.dynamic_slice_in_dim(positions, start, SLOT, 0)
            key_win = jnp.concatenate([lax.dynamic_slice_in_dim(key_wide, prev, SLOT, 0), lax.dynamic_slice_in_dim(key_wide, start, SLOT, 0)], axis=0)
            value_win = jnp.concatenate([lax.dynamic_slice_in_dim(value_wide, prev, SLOT, 0), lax.dynamic_slice_in_dim(value_wide, start, SLOT, 0)], axis=0)
            pos_win = jnp.concatenate([lax.dynamic_slice_in_dim(positions, prev, SLOT, 0), lax.dynamic_slice_in_dim(positions, start, SLOT, 0)], axis=0)
            scores = jnp.einsum('rgd,cd->grc', query_blk, key_win)
            visible = (pos_blk[:, None] >= pos_win[None, :])[None, :, :]
            probs = jnp.where(visible, jnp.exp(scores * factor - sums_blk.T[:, :, None]), 0.0)
            probs_low = probs.astype(jnp.bfloat16)
            d_probs = jnp.einsum('rgd,cd->grc', grad_blk, value_win)
            d_scores = (probs * (d_probs - delta_blk.T[:, :, None]) * factor).astype(jnp.bfloat16)
            value_terms = jnp.einsum('grc,rgd->cd', probs_low.astype(jnp.float32), grad_blk)
            key_terms = jnp.einsum('grc,rgd->cd', d_scores.astype(jnp.float32), query_blk)
            grad_query = jnp.einsum('grc,cd->rgd', d_scores.astype(jnp.float32), key_win)
            zero = jnp.zeros((), jnp.int32)
            key_gradient = lax.dynamic_update_slice(key_gradient, lax.dynamic_slice_in_dim(key_gradient, prev, SLOT, 0) + key_terms[:SLOT], (prev, zero))
            key_gradient = lax.dynamic_update_slice(key_gradient, lax.dynamic_slice_in_dim(key_gradient, start, SLOT, 0) + key_terms[SLOT:], (start, zero))
            value_gradient = lax.dynamic_update_slice(value_gradient, lax.dynamic_slice_in_dim(value_gradient, prev, SLOT, 0) + value_terms[:SLOT], (prev, zero))
            value_gradient = lax.dynamic_update_slice(value_gradient, lax.dynamic_slice_in_dim(value_gradient, start, SLOT, 0) + value_terms[SLOT:], (start, zero))
            return ((key_gradient, value_gradient), grad_query)
        slots = jnp.arange(N_BLK, dtype=jnp.int32)
        empty = jnp.zeros((SEQUENCE_LENGTH, HEAD_DIMENSION), jnp.float32)
        (key_gradient, value_gradient), grad_query = lax.scan(slot_step, (empty, empty), slots)
        return (grad_query.reshape(SEQUENCE_LENGTH, query_groups, HEAD_DIMENSION), key_gradient, value_gradient)
    grad_query, key_gradient, value_gradient = lax.map(per_head, (query_per_head, gradient_per_head, key_per_head, value_per_head, logsumexp_per_head, delta_per_head))
    grad_queries = grad_query.transpose(1, 0, 2, 3).reshape(SEQUENCE_LENGTH, QUERY_HEADS * HEAD_DIMENSION).astype(jnp.bfloat16)
    key_gradient = key_gradient.transpose(1, 0, 2).reshape(SEQUENCE_LENGTH, KEY_VALUE_HEADS * HEAD_DIMENSION).astype(jnp.bfloat16)
    value_gradient = value_gradient.transpose(1, 0, 2).reshape(SEQUENCE_LENGTH, KEY_VALUE_HEADS * HEAD_DIMENSION).astype(jnp.bfloat16)
    return (grad_queries, key_gradient, value_gradient)
```

```python
import functools
import math

import jax
import jax.numpy as jnp
from jax import lax
from jax.experimental import pallas as pl
from jax.experimental.pallas import tpu as pltpu
from jax.sharding import PartitionSpec as P

D = 128
N_ULY = 8
TOK = 128
GROUP = 4
HALF = 512
FACTOR = 1.0 / math.sqrt(D)
LOG2E = math.log2(math.e)
STAT = 32
BF = jnp.bfloat16
F32 = jnp.float32
MIB = 1 << 20


def nt(a, b):
    return lax.dot_general(a, b, (((1,), (1,)), ((), ())), preferred_element_type=F32)


def nn(a, b):
    return jnp.dot(a, b, preferred_element_type=F32)


def tn(a, b):
    return lax.dot_general(a, b, (((0,), (0,)), ((), ())), preferred_element_type=F32)


def pack_kernel(first, heads, with_kv, *refs):
    if with_kv:
        q_ref, do_ref, o_ref, lse_ref, k_ref, v_ref, msg_ref = refs
    else:
        q_ref, do_ref, o_ref, lse_ref, msg_ref = refs
    u = pl.program_id(0)
    lse_rows = jnp.transpose(lse_ref[...]) * LOG2E
    head_of = lax.broadcasted_iota(jnp.int32, lse_rows.shape, 0)
    row_of = lax.broadcasted_iota(jnp.int32, (8, D), 0)
    stats = jnp.zeros((8, TOK), F32)
    for j in range(heads):
        cols = slice(j * D, (j + 1) * D)
        msg_ref[0, j * TOK : (j + 1) * TOK, :] = q_ref[:, cols]
        msg_ref[0, (heads + j) * TOK : (heads + j + 1) * TOK, :] = do_ref[:, cols]
        product = do_ref[:, cols].astype(F32) * o_ref[:, cols].astype(F32)
        high = product.astype(BF)
        low = (product - high.astype(F32)).astype(BF)
        ones = jnp.where(row_of == heads + j, 1.0, 0.0).astype(BF)
        stats = stats + nt(ones, high) + nt(ones, low)
        lse_one = jnp.sum(
            jnp.where(head_of == u * GROUP + first + j, lse_rows, 0.0), axis=0, keepdims=True
        )
        stats = stats + jnp.where(row_of == j, lse_one, 0.0)
    at = 2 * heads * TOK
    if with_kv:
        msg_ref[0, at : at + TOK, :] = k_ref[...]
        msg_ref[0, at + TOK : at + 2 * TOK, :] = v_ref[...]
        at += 2 * TOK
    p0 = stats.astype(BF).astype(F32)
    p1 = (stats - p0).astype(BF).astype(F32)
    p2 = stats - p0 - p1
    pieces = jnp.concatenate([p0, p1, p2, jnp.zeros_like(p0)], axis=0)
    msg_ref[0, at : at + STAT, :] = pieces.astype(BF)


def pack(queries, grads, outputs, lse, kv, first, heads):
    rows = 2 * heads * TOK + STAT + (2 * TOK if kv else 0)
    per = GROUP // heads
    wide = pl.BlockSpec((TOK, heads * D), lambda u: (0, per * u + first // heads))
    one = pl.BlockSpec((TOK, D), lambda u: (0, u))
    return pl.pallas_call(
        functools.partial(pack_kernel, first, heads, bool(kv)),
        grid=(N_ULY,),
        in_specs=[wide, wide, wide, pl.BlockSpec(lse.shape, lambda u: (0, 0))] + [one] * len(kv),
        out_specs=pl.BlockSpec((1, rows, D), lambda u: (u, 0, 0)),
        out_shape=jax.ShapeDtypeStruct((N_ULY, rows, D), BF),
        name="pack_heads_%d" % first,
        cost_estimate=pl.CostEstimate(flops=10 * MIB, bytes_accessed=4 * MIB, transcendentals=0),
    )(queries, grads, outputs, lse, *kv)


def slots_of(order_ref):
    slot = lax.axis_index("blk")
    prev = lax.rem(slot + 15, 16)
    a, b = order_ref[slot, 0], order_ref[slot, 1]
    pa, pb = order_ref[prev, 0], order_ref[prev, 1]
    low = (a > b).astype(jnp.int32)
    prev_low = (pa > pb).astype(jnp.int32)
    lower_sees = jnp.minimum(a, b) > jnp.minimum(pa, pb)
    return low, prev_low, lower_sees


def half(ref, which, at):
    return ref[pl.ds(which * 4, 4), at : at + TOK, :].reshape(HALF, D)


def tile(q, do, lse, delta, k, v, shift):
    scores = nt(k, q)
    probs = jnp.exp2(scores * (FACTOR * LOG2E) - lse)
    if shift is not None:
        key = lax.broadcasted_iota(jnp.int32, probs.shape, 0)
        row = lax.broadcasted_iota(jnp.int32, probs.shape, 1)
        probs = jnp.where(row + shift >= key, probs, 0.0)
    d_probs = nt(v, do)
    d_scores = (probs * (d_probs - delta) * FACTOR).astype(BF)
    return nn(probs.astype(BF), do), nn(d_scores, q), tn(d_scores, k)


def stat_rows(x_ref, at):
    blocks = []
    for s in range(N_ULY):
        p = x_ref[s, at : at + STAT, :].astype(F32)
        blocks.append(p[0:8] + p[8:16] + p[16:24])
    return jnp.concatenate(blocks, axis=1)


def pick(stats, row, which):
    lower, upper = stats[row : row + 1, :HALF], stats[row : row + 1, HALF:]
    return jnp.where(which == 0, lower, upper)


def head_views(x_ref, stats, heads, j, which):
    return (
        half(x_ref, which, j * TOK),
        half(x_ref, which, (heads + j) * TOK),
        pick(stats, j, which),
        pick(stats, heads + j, which),
    )


def add_to(ref, index, which, value):
    ref[index, pl.ds(which * 4, 4)] += value.reshape(4, TOK, D)


def local_head(low, x_ref, stats, heads, j, k_ref, k_at, dq_ref, dkv_ref):
    high = 1 - low
    k_low, v_low = half(k_ref, low, k_at), half(k_ref, low, k_at + TOK)
    k_high, v_high = half(k_ref, high, k_at), half(k_ref, high, k_at + TOK)
    rows_low = head_views(x_ref, stats, heads, j, low)
    rows_high = head_views(x_ref, stats, heads, j, high)

    def diagonal(rows, k, v):
        q, do, lse, delta = rows
        dv0, dk0, dq0 = tile(q, do, lse, delta, k[:256], v[:256], 0)
        dv1, dk1, dq1 = tile(
            q[256:], do[256:], lse[:, 256:], delta[:, 256:], k[256:], v[256:], 0
        )
        dq = jnp.concatenate([dq0[:256], dq0[256:] + dq1], axis=0)
        return jnp.concatenate([dv0, dv1], 0), jnp.concatenate([dk0, dk1], 0), dq

    dv, dk, dq = tile(*rows_high, k_low, v_low, None)
    dv2, dk2, dq2 = diagonal(rows_high, k_high, v_high)
    add_to(dkv_ref, 0, high, dk2)
    add_to(dkv_ref, 1, high, dv2)
    dq_ref[pl.ds(high * 4, 4)] += (dq + dq2).reshape(4, TOK, D)
    dv3, dk3, dq3 = diagonal(rows_low, k_low, v_low)
    add_to(dkv_ref, 0, low, dk + dk3)
    add_to(dkv_ref, 1, low, dv + dv3)
    dq_ref[pl.ds(low * 4, 4)] += dq3.reshape(4, TOK, D)


def cross_head(low, prev_low, lower_sees, x_ref, stats, heads, j, kp_ref, dq_ref, dkv_ref):
    high = 1 - low
    k_low, v_low = half(kp_ref, prev_low, 0), half(kp_ref, prev_low, TOK)
    rows_high = head_views(x_ref, stats, heads, j, high)
    dv, dk, dq = tile(*rows_high, k_low, v_low, None)
    add_to(dkv_ref, 0, prev_low, dk)
    add_to(dkv_ref, 1, prev_low, dv)
    dq_ref[pl.ds(high * 4, 4)] += dq.reshape(4, TOK, D)
    sees = lower_sees.astype(jnp.int32)
    rows_at = sees * low + (1 - sees) * high
    keys_at = sees * prev_low + (1 - sees) * (1 - prev_low)
    k, v = half(kp_ref, keys_at, 0), half(kp_ref, keys_at, TOK)
    rows = head_views(x_ref, stats, heads, j, rows_at)
    dv, dk, dq = tile(*rows, k, v, None)
    add_to(dkv_ref, 0, keys_at, dk)
    add_to(dkv_ref, 1, keys_at, dv)
    dq_ref[pl.ds(rows_at * 4, 4)] += dq.reshape(4, TOK, D)


def first_kernel(heads, order_ref, x_ref, kp_ref, dq_out, local_out, cross_out, dq_acc):
    low, prev_low, lower_sees = slots_of(order_ref)
    kv_at = 2 * heads * TOK
    stats = stat_rows(x_ref, kv_at + 2 * TOK)
    local_out[...] = jnp.zeros_like(local_out)
    cross_out[...] = jnp.zeros_like(cross_out)
    for j in range(heads):
        dq_acc[...] = jnp.zeros_like(dq_acc)
        local_head(low, x_ref, stats, heads, j, x_ref, kv_at, dq_acc, local_out)
        cross_head(
            low, prev_low, lower_sees, x_ref, stats, heads, j, kp_ref, dq_acc, cross_out
        )
        dq_out[:, j * TOK : (j + 1) * TOK, :] = dq_acc[...].astype(BF)


def cross_kernel(heads, order_ref, x_ref, kp_ref, cross_in, dq_out, cross_out, acc):
    low, prev_low, lower_sees = slots_of(order_ref)
    stats = stat_rows(x_ref, 2 * heads * TOK)
    acc[...] = cross_in[...]
    dq_out[...] = jnp.zeros_like(dq_out)
    for j in range(heads):
        cross_head(
            low, prev_low, lower_sees, x_ref, stats, heads, j, kp_ref, dq_out.at[j], acc
        )
    cross_out[...] = acc[...].astype(BF)


def local_kernel(heads, kv_at, order_ref, x_ref, x0_ref, dq_in, local_in, dq_out, local_out, acc):
    low, _, _ = slots_of(order_ref)
    stats = stat_rows(x_ref, 2 * heads * TOK)
    local_out[...] = local_in[...]
    for j in range(heads):
        acc[...] = dq_in[j]
        local_head(low, x_ref, stats, heads, j, x0_ref, kv_at, acc, local_out)
        dq_out[:, j * TOK : (j + 1) * TOK, :] = acc[...].astype(BF)


def add_kernel(msg_in, local_ref, back_ref, msg_out):
    del msg_in
    total = local_ref[...] + back_ref[...].astype(F32)
    msg_out[:, 0:TOK, :] = total[0].astype(BF)
    msg_out[:, TOK : 2 * TOK, :] = total[1].astype(BF)


def unpack_kernel(heads, a_ref, b_ref, dq_ref, dk_ref, dv_ref):
    for j in range(heads):
        dq_ref[:, j * D : (j + 1) * D] = a_ref[0, j * TOK : (j + 1) * TOK, :]
        at = (heads + j) * D
        dq_ref[:, at : at + D] = b_ref[0, j * TOK : (j + 1) * TOK, :]
    dk_ref[...] = b_ref[0, heads * TOK : (heads + 1) * TOK, :]
    dv_ref[...] = b_ref[0, (heads + 1) * TOK : (heads + 2) * TOK, :]


def vmem():
    return pl.BlockSpec(memory_space=pltpu.VMEM)


def smem():
    return pl.BlockSpec(memory_space=pltpu.SMEM)


def params():
    return pltpu.CompilerParams(vmem_limit_bytes=40 * MIB)


def shift_slot(value, by):
    length = lax.axis_size("blk")
    return lax.ppermute(value, "blk", [(i, (i + by) % length) for i in range(length)])


def exchange(value):
    return lax.all_to_all(value, "uly", split_axis=0, concat_axis=0, tiled=True)


def body(queries, input_keys, input_values, outputs, output_gradient, saved_logsumexp, span_order):
    h = 2
    kv_at = 2 * h * TOK
    rows4 = (N_ULY, TOK, D)
    msg0 = pack(
        queries, output_gradient, outputs, saved_logsumexp, (input_keys, input_values), 0, h
    )
    x0 = exchange(msg0)
    msg1 = pack(queries, output_gradient, outputs, saved_logsumexp, (), h, h)
    x1 = exchange(msg1)
    kv_prev = shift_slot(x0[:, kv_at : kv_at + 2 * TOK, :], 1)

    def cost(units):
        return pl.CostEstimate(
            flops=units * h * 5 * 2 * 512 * 512 * 128 * 2,
            bytes_accessed=4 * MIB,
            transcendentals=units * h * 512 * 512,
        )

    dq0, local, cross = pl.pallas_call(
        functools.partial(first_kernel, h),
        in_specs=[smem(), vmem(), vmem()],
        out_specs=[vmem()] * 3,
        out_shape=[
            jax.ShapeDtypeStruct((N_ULY, h * TOK, D), BF),
            jax.ShapeDtypeStruct((2,) + rows4, F32),
            jax.ShapeDtypeStruct((2,) + rows4, F32),
        ],
        scratch_shapes=[pltpu.VMEM(rows4, F32)],
        compiler_params=params(),
        cost_estimate=cost(5),
        name="first_heads",
    )(span_order, x0, kv_prev)
    r0 = exchange(dq0)
    dq1, cross_low = pl.pallas_call(
        functools.partial(cross_kernel, h),
        in_specs=[smem(), vmem(), vmem(), vmem()],
        out_specs=[vmem()] * 2,
        out_shape=[
            jax.ShapeDtypeStruct((h,) + rows4, F32),
            jax.ShapeDtypeStruct((2,) + rows4, BF),
        ],
        scratch_shapes=[pltpu.VMEM((2,) + rows4, F32)],
        compiler_params=params(),
        cost_estimate=cost(2),
        name="cross_heads",
    )(span_order, x1, kv_prev, cross)
    back = shift_slot(cross_low, -1)
    dq1, local = pl.pallas_call(
        functools.partial(local_kernel, h, kv_at),
        in_specs=[smem()] + [vmem()] * 4,
        out_specs=[vmem()] * 2,
        out_shape=[
            jax.ShapeDtypeStruct((N_ULY, h * TOK, D), BF),
            jax.ShapeDtypeStruct((2,) + rows4, F32),
        ],
        scratch_shapes=[pltpu.VMEM(rows4, F32)],
        compiler_params=params(),
        cost_estimate=cost(3),
        name="local_heads",
    )(span_order, x1, x0, dq1, local)
    dkv = (local + back.astype(F32)).astype(BF)
    msg = jnp.concatenate([dq1, dkv[0], dkv[1]], axis=1)
    r1 = exchange(msg)
    return pl.pallas_call(
        functools.partial(unpack_kernel, h),
        grid=(N_ULY,),
        in_specs=[
            pl.BlockSpec((1, h * TOK, D), lambda u: (u, 0, 0)),
            pl.BlockSpec((1, (h + 2) * TOK, D), lambda u: (u, 0, 0)),
        ],
        out_specs=[
            pl.BlockSpec((TOK, GROUP * D), lambda u: (0, u)),
            pl.BlockSpec((TOK, D), lambda u: (0, u)),
            pl.BlockSpec((TOK, D), lambda u: (0, u)),
        ],
        out_shape=[
            jax.ShapeDtypeStruct((TOK, N_ULY * GROUP * D), BF),
            jax.ShapeDtypeStruct((TOK, N_ULY * D), BF),
            jax.ShapeDtypeStruct((TOK, N_ULY * D), BF),
        ],
        name="unpack",
    )(r0, r1)


def solution(mesh):
    rows = P(("blk", "uly"), None)
    return jax.shard_map(
        body, mesh=mesh, in_specs=(rows,) * 6 + (P(),), out_specs=(rows,) * 3, check_vma=False
    )
```

```python
import functools
import math

import jax
import jax.numpy as jnp
from jax import lax
from jax.experimental import pallas as pl
from jax.experimental.pallas import tpu as pltpu
from jax.sharding import PartitionSpec as P

D = 128
N_ULY = 8
TOK = 128
GROUP = 4
HALF = 512
FACTOR = 1.0 / math.sqrt(D)
LOG2E = math.log2(math.e)
STAT = 32
BF = jnp.bfloat16
F32 = jnp.float32
MIB = 1 << 20


def nt(a, b):
    return lax.dot_general(a, b, (((1,), (1,)), ((), ())), preferred_element_type=F32)


def nn(a, b):
    return jnp.dot(a, b, preferred_element_type=F32)


def tn(a, b):
    return lax.dot_general(a, b, (((0,), (0,)), ((), ())), preferred_element_type=F32)


def copy_of(source, target, sem):
    return pltpu.make_async_copy(source, target, sem)


def head_group(u):
    upper = lax.axis_index("blk") // 8
    return u + upper * (1 - 2 * (u % 2))


def pack_kernel(first, heads, with_kv, *refs):
    if with_kv:
        q_ref, do_ref, o_ref, lse_hbm, k_ref, v_ref, msg_ref, buf, o_buf, lse_ref, sem = refs
    else:
        q_ref, do_ref, o_ref, lse_hbm, msg_ref, buf, o_buf, lse_ref, sem = refs
    rows = 2 * heads * TOK + (2 * TOK if with_kv else 0)
    lse_load = copy_of(lse_hbm, lse_ref, sem.at[3, 0])
    lse_load.start()

    for u in range(N_ULY):
        group = head_group(u)

        def load(source, column, at):
            cols = pl.ds(pl.multiple_of(column * D, D), D)
            copy_of(source.at[:, cols], buf.at[u, pl.ds(at, TOK), :], sem.at[0, u]).start()

        o_cols = pl.ds(pl.multiple_of((group * GROUP + first) * D, D), heads * D)
        copy_of(o_ref.at[:, o_cols], o_buf.at[u], sem.at[1, u]).start()
        for j in range(heads):
            load(do_ref, group * GROUP + first + j, (heads + j) * TOK)
        for j in range(heads):
            load(q_ref, group * GROUP + first + j, j * TOK)
        if with_kv:
            load(k_ref, group, 2 * heads * TOK)
            load(v_ref, group, (2 * heads + 1) * TOK)
    row_of = lax.broadcasted_iota(jnp.int32, (8, D), 0)
    lse_load.wait()
    for u in range(N_ULY):
        loaded = buf.at[u, pl.ds(0, rows), :]
        copy_of(loaded, loaded, sem.at[0, u]).wait()
        copy_of(o_buf.at[u], o_buf.at[u], sem.at[1, u]).wait()
        at = head_group(u) * GROUP + first
        stats = jnp.zeros((8, TOK), F32)
        for j in range(heads):
            grads = buf[u, (heads + j) * TOK : (heads + j + 1) * TOK, :].astype(F32)
            product = grads * o_buf[u, :, j * D : (j + 1) * D].astype(F32)
            high = product.astype(BF)
            low = (product - high.astype(F32)).astype(BF)
            ones = jnp.where(row_of == heads + j, 1.0, 0.0).astype(BF)
            stats = stats + nt(ones, high) + nt(ones, low)
            lse_one = lse_ref[pl.ds(at + j, 1), :] * LOG2E
            stats = stats + jnp.where(row_of == j, lse_one, 0.0)
        p0 = stats.astype(BF).astype(F32)
        p1 = (stats - p0).astype(BF).astype(F32)
        p2 = stats - p0 - p1
        pieces = jnp.concatenate([p0, p1, p2, jnp.zeros_like(p0)], axis=0)
        buf[u, rows : rows + STAT, :] = pieces.astype(BF)
        copy_of(buf.at[u], msg_ref.at[u], sem.at[2, u]).start()
    for u in range(N_ULY):
        copy_of(buf.at[u], msg_ref.at[u], sem.at[2, u]).wait()


def pack(queries, grads, outputs, lse, kv, first, heads):
    rows = 2 * heads * TOK + STAT + (2 * TOK if kv else 0)
    message = ((N_ULY, rows, D), BF)
    (msg,) = call(
        functools.partial(pack_kernel, first, heads, bool(kv)),
        [(array, pltpu.HBM) for array in (queries, grads, outputs, lse) + kv],
        ((message, pltpu.HBM),),
        [
            pltpu.VMEM(*message),
            pltpu.VMEM((N_ULY, TOK, heads * D), BF),
            pltpu.VMEM(lse.shape, F32),
            pltpu.SemaphoreType.DMA((4, N_ULY)),
        ],
        1,
        "pack_heads_%d" % first,
    )
    return msg


def slots_of(order_ref):
    slot = lax.axis_index("blk")
    prev = lax.rem(slot + 15, 16)
    a, b = order_ref[0, slot], order_ref[1, slot]
    pa, pb = order_ref[0, prev], order_ref[1, prev]
    low = (a > b).astype(jnp.int32)
    prev_low = (pa > pb).astype(jnp.int32)
    lower_sees = jnp.minimum(a, b) > jnp.minimum(pa, pb)
    return low, prev_low, lower_sees


def half(ref, which, at):
    return ref[pl.ds(which * 4, 4), at : at + TOK, :].reshape(HALF, D)


def tile(rows, k, v, heads=None):
    q, do, lse, delta = rows
    probs = jnp.exp2(nt(k, q) * (FACTOR * LOG2E) - lse)
    if heads is not None:
        key = lax.broadcasted_iota(jnp.int32, probs.shape, 0)
        row = lax.broadcasted_iota(jnp.int32, probs.shape, 1) % (probs.shape[1] // heads)
        probs = jnp.where(row >= key, probs, 0.0)
    d_scores = (probs * (nt(v, do) - delta) * FACTOR).astype(BF)
    return nn(probs.astype(BF), do), nn(d_scores, q), tn(d_scores, k)


def stat_rows(x_ref, at):
    blocks = []
    for s in range(N_ULY):
        p = x_ref[s, at : at + STAT, :].astype(F32)
        blocks.append(p[0:8] + p[8:16] + p[16:24])
    return jnp.concatenate(blocks, axis=1)


def pick(stats, row, which):
    lower, upper = stats[row : row + 1, :HALF], stats[row : row + 1, HALF:]
    return jnp.where(which == 0, lower, upper)


def rows_of(x_ref, stats, heads, which):
    def join(at):
        return jnp.concatenate([half(x_ref, which, (at + j) * TOK) for j in range(heads)], axis=0)

    def join_stats(at):
        return jnp.concatenate([pick(stats, at + j, which) for j in range(heads)], axis=1)

    return join(0), join(heads), join_stats(0), join_stats(heads)


def upper_rows(rows, heads):
    q, do, lse, delta = rows
    q, do = [
        jnp.concatenate([a[j * HALF + 256 : (j + 1) * HALF] for j in range(heads)], 0)
        for a in (q, do)
    ]
    lse, delta = [
        jnp.concatenate([a[:, j * HALF + 256 : (j + 1) * HALF] for j in range(heads)], 1)
        for a in (lse, delta)
    ]
    return q, do, lse, delta


def diagonal(rows, k, v, heads):
    dv0, dk0, dq0 = tile(rows, k[:256], v[:256], heads)
    dv1, dk1, dq1 = tile(upper_rows(rows, heads), k[256:], v[256:], heads)
    dq = []
    for j in range(heads):
        at = j * HALF
        dq.append(dq0[at : at + 256])
        dq.append(dq0[at + 256 : at + HALF] + dq1[j * 256 : (j + 1) * 256])
    return (
        jnp.concatenate([dv0, dv1], 0),
        jnp.concatenate([dk0, dk1], 0),
        jnp.concatenate(dq, 0),
    )


def blocks(value):
    return value.reshape(4, TOK, D)


def put(ref, index, which, value, add=False):
    at = (index, pl.ds(which * 4, 4))
    ref[at] = ref[at] + blocks(value) if add else blocks(value)


def put_heads(ref, heads, which, value, add=False):
    for j in range(heads):
        put(ref, j, which, value[j * HALF : (j + 1) * HALF], add)


def local_tiles(low, x_ref, stats, heads, k_ref, k_at, dq, dkv, after_high):
    high = 1 - low
    k_low, v_low = half(k_ref, low, k_at), half(k_ref, low, k_at + TOK)
    k_high, v_high = half(k_ref, high, k_at), half(k_ref, high, k_at + TOK)
    rows_high = rows_of(x_ref, stats, heads, high)
    rows_low = rows_of(x_ref, stats, heads, low)
    dv2, dk2, dq2 = diagonal(rows_high, k_high, v_high, heads)
    put(dkv, 0, high, dk2)
    put(dkv, 1, high, dv2)
    after_high(high)
    dv, dk, dq1 = tile(rows_high, k_low, v_low)
    put_heads(dq, heads, high, dq1 + dq2)
    dv3, dk3, dq3 = diagonal(rows_low, k_low, v_low, heads)
    put(dkv, 0, low, dk + dk3)
    put(dkv, 1, low, dv + dv3)
    put_heads(dq, heads, low, dq3)


def cross_tiles(low, prev_low, lower_sees, x_ref, stats, heads, kp_ref, dq, dkv):
    high, prev_high = 1 - low, 1 - prev_low
    k, v = half(kp_ref, prev_low, 0), half(kp_ref, prev_low, TOK)
    dv, dk, dq_high = tile(rows_of(x_ref, stats, heads, high), k, v)
    put(dkv, 0, prev_low, dk)
    put(dkv, 1, prev_low, dv)
    put_heads(dq, heads, high, dq_high)
    dkv[:, pl.ds(prev_high * 4, 4)] = jnp.zeros((2, 4, TOK, D), F32)
    dq[:, pl.ds(low * 4, 4)] = jnp.zeros((heads, 4, TOK, D), F32)
    sees = lower_sees.astype(jnp.int32)
    rows_at = sees * low + (1 - sees) * high
    keys_at = sees * prev_low + (1 - sees) * prev_high
    k, v = half(kp_ref, keys_at, 0), half(kp_ref, keys_at, TOK)
    dv, dk, dq_two = tile(rows_of(x_ref, stats, heads, rows_at), k, v)
    put(dkv, 0, keys_at, dk, True)
    put(dkv, 1, keys_at, dv, True)
    put_heads(dq, heads, rows_at, dq_two, True)


def local0_kernel(heads, order_ref, x_hbm, x_ref, dq_out, local_hbm, dkv, sem):
    low, _, _ = slots_of(order_ref)
    load = copy_of(x_hbm, x_ref, sem.at[0])
    load.start()
    load.wait()
    kv_at = 2 * heads * TOK
    stats = stat_rows(x_ref, kv_at + 2 * TOK)

    def store(which, number):
        part = pl.ds(which * 4, 4)
        return copy_of(dkv.at[:, part], local_hbm.at[:, part], sem.at[number])

    local_tiles(
        low, x_ref, stats, heads, x_ref, kv_at, dq_out, dkv, lambda high: store(high, 1).start()
    )
    store(low, 2).start()
    store(1 - low, 1).wait()
    store(low, 2).wait()


def cross0_kernel(heads, order_ref, x_ref, kp_ref, dq_in, msg_hbm, cross_hbm, dq, dkv, out, sem):
    low, prev_low, lower_sees = slots_of(order_ref)
    stats = stat_rows(x_ref, (2 * heads + 2) * TOK)
    cross_tiles(low, prev_low, lower_sees, x_ref, stats, heads, kp_ref, dq, dkv)
    store = copy_of(dkv, cross_hbm, sem.at[0])
    store.start()
    for j in range(heads):
        out[:, j * TOK : (j + 1) * TOK, :] = (dq[j] + dq_in[j]).astype(BF)
    send = copy_of(out, msg_hbm.at[:, pl.ds(0, heads * TOK), :], sem.at[1])
    send.start()
    store.wait()
    send.wait()


def cross1_kernel(
    heads, order_ref, x_hbm, kp_ref, cross_hbm, dq_hbm, cross_out, x_ref, dq, dkv, held, sem
):
    low, prev_low, lower_sees = slots_of(order_ref)
    load = copy_of(x_hbm, x_ref, sem.at[0])
    held_load = copy_of(cross_hbm, held, sem.at[1])
    load.start()
    held_load.start()
    load.wait()
    stats = stat_rows(x_ref, 2 * heads * TOK)
    cross_tiles(low, prev_low, lower_sees, x_ref, stats, heads, kp_ref, dq, dkv)
    store = copy_of(dq, dq_hbm, sem.at[2])
    store.start()
    held_load.wait()
    cross_out[...] = (dkv[...] + held[...]).astype(BF)
    store.wait()


def local1_kernel(
    heads, kv_at, order_ref, x_hbm, x0_hbm, dq_hbm, local_hbm, msg_in, msg_hbm, local_out,
    x_ref, kv_ref, dq, dq_held, held, out, sem,
):
    del msg_in
    low, _, _ = slots_of(order_ref)
    load = copy_of(x_hbm, x_ref, sem.at[0])
    kv_load = copy_of(x0_hbm.at[:, pl.ds(kv_at, 2 * TOK), :], kv_ref, sem.at[1])
    dq_load = copy_of(dq_hbm, dq_held, sem.at[2])
    held_load = copy_of(local_hbm, held, sem.at[3])
    for one in (load, kv_load, dq_load, held_load):
        one.start()
    load.wait()
    kv_load.wait()
    stats = stat_rows(x_ref, 2 * heads * TOK)
    local_tiles(low, x_ref, stats, heads, kv_ref, 0, dq, local_out, lambda high: None)
    dq_load.wait()
    for j in range(heads):
        out[:, j * TOK : (j + 1) * TOK, :] = (dq[j] + dq_held[j]).astype(BF)
    send = copy_of(out, msg_hbm.at[:, pl.ds(heads * TOK, heads * TOK), :], sem.at[4])
    send.start()
    held_load.wait()
    local_out[...] += held[...]
    send.wait()


def add_kernel(heads, local_ref, back_ref, msg_in, msg_hbm, out, sem):
    del msg_in
    for i in range(2):
        total = local_ref[i] + back_ref[i].astype(F32)
        out[:, i * TOK : (i + 1) * TOK, :] = total.astype(BF)
    send = copy_of(out, msg_hbm.at[:, pl.ds(2 * heads * TOK, 2 * TOK), :], sem.at[0])
    send.start()
    send.wait()


def unpack_kernel(x_hbm, dq_ref, dk_ref, dv_ref, buf, in_sem, sem):
    loads = [copy_of(x_hbm.at[u], buf.at[u], in_sem.at[u]) for u in range(N_ULY)]
    for load in loads:
        load.start()

    def store(u, at, target, column, which):
        cols = pl.ds(pl.multiple_of(column * D, D), D)
        copy_of(buf.at[u, pl.ds(at, TOK), :], target.at[:, cols], sem.at[which]).start()

    for u in range(N_ULY):
        group = head_group(u)
        loads[u].wait()
        for j in range(GROUP):
            store(u, j * TOK, dq_ref, group * GROUP + j, 0)
        store(u, GROUP * TOK, dk_ref, group, 1)
        store(u, (GROUP + 1) * TOK, dv_ref, group, 2)
    for which, ref in enumerate((dq_ref, dk_ref, dv_ref)):
        copy_of(ref, ref, sem.at[which]).wait()


def params():
    return pltpu.CompilerParams(vmem_limit_bytes=32 * MIB)


def shift_slot(value, by):
    pairs = []
    for slot in range(16):
        other = (slot + by) % 16
        flip = 1 if slot // 8 != other // 8 else 0
        pairs += [(slot * N_ULY + u, other * N_ULY + (u ^ flip)) for u in range(N_ULY)]
    return lax.ppermute(value, ("blk", "uly"), pairs)


def exchange(value):
    return lax.all_to_all(value, "uly", split_axis=0, concat_axis=0, tiled=True)


def call(kernel, inputs, outs, scratch, units, name, aliases=None):
    def placed(array, space):
        return pltpu.with_memory_space_constraint(array, space) if space == pltpu.HBM else array

    def shaped(shape, space):
        return pltpu.HBM(*shape) if space == pltpu.HBM else jax.ShapeDtypeStruct(*shape)

    return pl.pallas_call(
        kernel,
        in_specs=[pl.BlockSpec(memory_space=space) for _, space in inputs],
        out_specs=[pl.BlockSpec(memory_space=space) for _, space in outs],
        out_shape=[shaped(shape, space) for shape, space in outs],
        scratch_shapes=scratch,
        input_output_aliases=aliases or {},
        compiler_params=params(),
        cost_estimate=pl.CostEstimate(
            flops=units * 5 * 2 * 512 * 512 * 128 * 2,
            bytes_accessed=4 * MIB,
            transcendentals=units * 512 * 512,
        ),
        name=name,
    )(*[placed(array, space) for array, space in inputs])


def body(queries, input_keys, input_values, outputs, output_gradient, saved_logsumexp, span_order):
    h = 2
    kv_at = 2 * h * TOK
    rows4 = (N_ULY, TOK, D)
    lse = saved_logsumexp.T
    order = (span_order.T, pltpu.SMEM)
    msg0 = pack(queries, output_gradient, outputs, lse, (input_keys, input_values), 0, h)
    x0 = exchange(msg0)
    msg1 = pack(queries, output_gradient, outputs, lse, (), h, h)
    x0, msg1 = lax.optimization_barrier((x0, msg1))
    x1 = exchange(msg1)
    kv_prev = shift_slot(x0[:, kv_at : kv_at + 2 * TOK, :], 1)

    vmem, hbm = pltpu.VMEM, pltpu.HBM
    head_sums = ((h,) + rows4, F32)
    pair_sums = ((2,) + rows4, F32)
    pair_low = ((2,) + rows4, BF)
    head_low = ((N_ULY, h * TOK, D), BF)
    message = ((N_ULY, (GROUP + 2) * TOK, D), BF)
    sems = pltpu.SemaphoreType.DMA((5,))
    x0_near, dq0, local = call(
        functools.partial(local0_kernel, h),
        (order, (x0, hbm)),
        (((x0.shape, BF), vmem), (head_sums, vmem), (pair_sums, hbm)),
        [pltpu.VMEM(*pair_sums), sems],
        3 * h,
        "local_first",
    )
    msg, cross = call(
        functools.partial(cross0_kernel, h),
        (order, (x0_near, vmem), (kv_prev, vmem), (dq0, vmem)),
        ((message, hbm), (pair_sums, hbm)),
        [pltpu.VMEM(*head_sums), pltpu.VMEM(*pair_sums), pltpu.VMEM(*head_low), sems],
        2 * h,
        "cross_first",
    )
    dq1, cross_low = call(
        functools.partial(cross1_kernel, h),
        (order, (x1, hbm), (kv_prev, vmem), (cross, hbm)),
        ((head_sums, hbm), (pair_low, vmem)),
        [
            pltpu.VMEM(x1.shape, BF),
            pltpu.VMEM(*head_sums),
            pltpu.VMEM(*pair_sums),
            pltpu.VMEM(*pair_sums),
            sems,
        ],
        2 * h,
        "cross_last",
    )
    back = shift_slot(cross_low, -1)
    msg, local = call(
        functools.partial(local1_kernel, h, kv_at),
        (order, (x1, hbm), (x0, hbm), (dq1, hbm), (local, hbm), (msg, hbm)),
        ((message, hbm), (pair_sums, vmem)),
        [
            pltpu.VMEM(x1.shape, BF),
            pltpu.VMEM((N_ULY, 2 * TOK, D), BF),
            pltpu.VMEM(*head_sums),
            pltpu.VMEM(*head_sums),
            pltpu.VMEM(*pair_sums),
            pltpu.VMEM(*head_low),
            sems,
        ],
        3 * h,
        "local_last",
        {5: 0},
    )
    (msg,) = call(
        functools.partial(add_kernel, h),
        ((local, vmem), (back, vmem), (msg, hbm)),
        ((message, hbm),),
        [pltpu.VMEM((N_ULY, 2 * TOK, D), BF), sems],
        0,
        "add_returned",
        {2: 0},
    )
    result = exchange(msg)
    return call(
        unpack_kernel,
        ((result, hbm),),
        (
            (((TOK, N_ULY * GROUP * D), BF), hbm),
            (((TOK, N_ULY * D), BF), hbm),
            (((TOK, N_ULY * D), BF), hbm),
        ),
        [
            pltpu.VMEM(*message),
            pltpu.SemaphoreType.DMA((N_ULY,)),
            pltpu.SemaphoreType.DMA((3,)),
        ],
        0,
        "unpack",
    )


def solution(mesh):
    rows = P(("blk", "uly"), None)
    return jax.shard_map(
        body, mesh=mesh, in_specs=(rows,) * 6 + (P(),), out_specs=(rows,) * 3, check_vma=False
    )
```

```python
import functools
import math

import jax
import jax.numpy as jnp
from jax import lax
from jax.experimental import pallas as pl
from jax.experimental.pallas import tpu as pltpu
from jax.sharding import PartitionSpec as P

D = 128
N_ULY = 8
TOK = 128
GROUP = 4
HALF = 512
FACTOR = 1.0 / math.sqrt(D)
LOG2E = math.log2(math.e)
STAT = 32
BF = jnp.bfloat16
F32 = jnp.float32
MIB = 1 << 20
ORDERS = ((0, 2, 4, 6, 1, 3, 5, 7), (7, 6, 5, 4, 3, 2, 1, 0))
PLACES = tuple(tuple(order.index(u) for u in range(N_ULY)) for order in ORDERS)


def parity():
    return lax.axis_index("blk") % 2


def choose(table, index, odd):
    return table[0][index] + odd * (table[1][index] - table[0][index])


def device_at(place):
    return choose(ORDERS, place, parity())


def place_of(u):
    return choose(PLACES, u, parity())


def nt(a, b):
    return lax.dot_general(a, b, (((1,), (1,)), ((), ())), preferred_element_type=F32)


def nn(a, b):
    return jnp.dot(a, b, preferred_element_type=F32)


def tn(a, b):
    return lax.dot_general(a, b, (((0,), (0,)), ((), ())), preferred_element_type=F32)


def copy_of(source, target, sem):
    return pltpu.make_async_copy(source, target, sem)


def head_group(u):
    upper = lax.axis_index("blk") // 8
    return u ^ upper


def pack_kernel(first, heads, with_kv, *refs):
    if with_kv:
        q_ref, do_ref, o_ref, lse_hbm, k_ref, v_ref, msg_ref, buf, o_buf, lse_ref, sem = refs
    else:
        q_ref, do_ref, o_ref, lse_hbm, msg_ref, buf, o_buf, lse_ref, sem = refs
    rows = 2 * heads * TOK + (2 * TOK if with_kv else 0)
    lse_load = copy_of(lse_hbm, lse_ref, sem.at[3, 0])
    lse_load.start()

    groups = [head_group(device_at(i)) for i in range(N_ULY)]
    for u, group in enumerate(groups):

        def load(source, column, at):
            cols = pl.ds(pl.multiple_of(column * D, D), D)
            copy_of(source.at[:, cols], buf.at[u, pl.ds(at, TOK), :], sem.at[0, u]).start()

        o_cols = pl.ds(pl.multiple_of((group * GROUP + first) * D, D), heads * D)
        copy_of(o_ref.at[:, o_cols], o_buf.at[u], sem.at[1, u]).start()
        for j in range(heads):
            load(do_ref, group * GROUP + first + j, (heads + j) * TOK)
        for j in range(heads):
            load(q_ref, group * GROUP + first + j, j * TOK)
        if with_kv:
            load(k_ref, group, 2 * heads * TOK)
            load(v_ref, group, (2 * heads + 1) * TOK)
    row_of = lax.broadcasted_iota(jnp.int32, (8, D), 0)
    lse_load.wait()
    for u in range(N_ULY):
        loaded = buf.at[u, pl.ds(0, rows), :]
        copy_of(loaded, loaded, sem.at[0, u]).wait()
        copy_of(o_buf.at[u], o_buf.at[u], sem.at[1, u]).wait()
        at = groups[u] * GROUP + first
        stats = jnp.zeros((8, TOK), F32)
        for j in range(heads):
            grads = buf[u, (heads + j) * TOK : (heads + j + 1) * TOK, :].astype(F32)
            product = grads * o_buf[u, :, j * D : (j + 1) * D].astype(F32)
            high = product.astype(BF)
            low = (product - high.astype(F32)).astype(BF)
            ones = jnp.where(row_of == heads + j, 1.0, 0.0).astype(BF)
            stats = stats + nt(ones, high) + nt(ones, low)
            lse_one = lse_ref[pl.ds(at + j, 1), :] * LOG2E
            stats = stats + jnp.where(row_of == j, lse_one, 0.0)
        p0 = stats.astype(BF).astype(F32)
        p1 = (stats - p0).astype(BF).astype(F32)
        p2 = stats - p0 - p1
        pieces = jnp.concatenate([p0, p1, p2, jnp.zeros_like(p0)], axis=0)
        buf[u, rows : rows + STAT, :] = pieces.astype(BF)
        copy_of(buf.at[u], msg_ref.at[u], sem.at[2, u]).start()
    for u in range(N_ULY):
        copy_of(buf.at[u], msg_ref.at[u], sem.at[2, u]).wait()


def pack(queries, grads, outputs, lse, kv, first, heads):
    rows = 2 * heads * TOK + STAT + (2 * TOK if kv else 0)
    message = ((N_ULY, rows, D), BF)
    (msg,) = call(
        functools.partial(pack_kernel, first, heads, bool(kv)),
        [(array, pltpu.HBM) for array in (queries, grads, outputs, lse) + kv],
        ((message, pltpu.HBM),),
        [
            pltpu.VMEM(*message),
            pltpu.VMEM((N_ULY, TOK, heads * D), BF),
            pltpu.VMEM(lse.shape, F32),
            pltpu.SemaphoreType.DMA((4, N_ULY)),
        ],
        1,
        "pack_heads_%d" % first,
    )
    return msg


def slots_of(order_ref):
    slot = lax.axis_index("blk")
    prev = lax.rem(slot + 15, 16)
    a, b = order_ref[0, slot], order_ref[1, slot]
    pa, pb = order_ref[0, prev], order_ref[1, prev]
    low = (a > b).astype(jnp.int32)
    prev_low = (pa > pb).astype(jnp.int32)
    lower_sees = jnp.minimum(a, b) > jnp.minimum(pa, pb)
    return low, prev_low, lower_sees


def half(ref, which, at, odd=None):
    odd = parity() if odd is None else odd
    parts = []
    for b in range(4):
        lower, upper = choose(PLACES, b, odd), choose(PLACES, 4 + b, odd)
        parts.append(ref[lower + which * (upper - lower), at : at + TOK, :])
    return jnp.concatenate(parts, axis=0)


def tile(rows, k, v, heads=None):
    q, do, lse, delta = rows
    probs = jnp.exp2(nt(k, q) * (FACTOR * LOG2E) - lse)
    if heads is not None:
        key = lax.broadcasted_iota(jnp.int32, probs.shape, 0)
        row = lax.broadcasted_iota(jnp.int32, probs.shape, 1) % (probs.shape[1] // heads)
        probs = jnp.where(row >= key, probs, 0.0)
    d_scores = (probs * (nt(v, do) - delta) * FACTOR).astype(BF)
    return nn(probs.astype(BF), do), nn(d_scores, q), tn(d_scores, k)


def stat_rows(x_ref, at):
    blocks = []
    for s in range(N_ULY):
        p = x_ref[place_of(s), at : at + STAT, :].astype(F32)
        blocks.append(p[0:8] + p[8:16] + p[16:24])
    return jnp.concatenate(blocks, axis=1)


def pick(stats, row, which):
    lower, upper = stats[row : row + 1, :HALF], stats[row : row + 1, HALF:]
    return jnp.where(which == 0, lower, upper)


def rows_of(x_ref, stats, heads, which):
    def join(at):
        return jnp.concatenate([half(x_ref, which, (at + j) * TOK) for j in range(heads)], axis=0)

    def join_stats(at):
        return jnp.concatenate([pick(stats, at + j, which) for j in range(heads)], axis=1)

    return join(0), join(heads), join_stats(0), join_stats(heads)


def upper_rows(rows, heads):
    q, do, lse, delta = rows
    q, do = [
        jnp.concatenate([a[j * HALF + 256 : (j + 1) * HALF] for j in range(heads)], 0)
        for a in (q, do)
    ]
    lse, delta = [
        jnp.concatenate([a[:, j * HALF + 256 : (j + 1) * HALF] for j in range(heads)], 1)
        for a in (lse, delta)
    ]
    return q, do, lse, delta


def diagonal(rows, k, v, heads):
    dv0, dk0, dq0 = tile(rows, k[:256], v[:256], heads)
    dv1, dk1, dq1 = tile(upper_rows(rows, heads), k[256:], v[256:], heads)
    dq = []
    for j in range(heads):
        at = j * HALF
        dq.append(dq0[at : at + 256])
        dq.append(dq0[at + 256 : at + HALF] + dq1[j * 256 : (j + 1) * 256])
    return (
        jnp.concatenate([dv0, dv1], 0),
        jnp.concatenate([dk0, dk1], 0),
        jnp.concatenate(dq, 0),
    )


def blocks(value):
    return value.reshape(4, TOK, D)


def put(ref, index, which, value, add=False):
    at = (index, pl.ds(which * 4, 4))
    ref[at] = ref[at] + blocks(value) if add else blocks(value)


def put_heads(ref, heads, which, value, add=False):
    for j in range(heads):
        put(ref, j, which, value[j * HALF : (j + 1) * HALF], add)


def local_tiles(low, x_ref, stats, heads, k_ref, k_at, dq, dkv, after_high):
    high = 1 - low
    k_low, v_low = half(k_ref, low, k_at), half(k_ref, low, k_at + TOK)
    k_high, v_high = half(k_ref, high, k_at), half(k_ref, high, k_at + TOK)
    rows_high = rows_of(x_ref, stats, heads, high)
    rows_low = rows_of(x_ref, stats, heads, low)
    dv2, dk2, dq2 = diagonal(rows_high, k_high, v_high, heads)
    put(dkv, 0, high, dk2)
    put(dkv, 1, high, dv2)
    after_high(high)
    dv, dk, dq1 = tile(rows_high, k_low, v_low)
    put_heads(dq, heads, high, dq1 + dq2)
    dv3, dk3, dq3 = diagonal(rows_low, k_low, v_low, heads)
    put(dkv, 0, low, dk + dk3)
    put(dkv, 1, low, dv + dv3)
    put_heads(dq, heads, low, dq3)


def cross_tiles(low, prev_low, lower_sees, x_ref, stats, heads, kp_ref, dq, dkv):
    high, prev_high = 1 - low, 1 - prev_low
    odd = 1 - parity()
    k, v = half(kp_ref, prev_low, 0, odd), half(kp_ref, prev_low, TOK, odd)
    dv, dk, dq_high = tile(rows_of(x_ref, stats, heads, high), k, v)
    put(dkv, 0, prev_low, dk)
    put(dkv, 1, prev_low, dv)
    put_heads(dq, heads, high, dq_high)
    dkv[:, pl.ds(prev_high * 4, 4)] = jnp.zeros((2, 4, TOK, D), F32)
    dq[:, pl.ds(low * 4, 4)] = jnp.zeros((heads, 4, TOK, D), F32)
    sees = lower_sees.astype(jnp.int32)
    rows_at = sees * low + (1 - sees) * high
    keys_at = sees * prev_low + (1 - sees) * prev_high
    k, v = half(kp_ref, keys_at, 0, odd), half(kp_ref, keys_at, TOK, odd)
    dv, dk, dq_two = tile(rows_of(x_ref, stats, heads, rows_at), k, v)
    put(dkv, 0, keys_at, dk, True)
    put(dkv, 1, keys_at, dv, True)
    put_heads(dq, heads, rows_at, dq_two, True)


def send_rows(out, msg_hbm, at, sem):
    rows = out.shape[1]
    for u in range(N_ULY):
        copy_of(out.at[u], msg_hbm.at[place_of(u), pl.ds(at, rows), :], sem).start()
    return copy_of(out, out, sem)


def local0_kernel(heads, order_ref, x_ref, dq_out, local_hbm, dkv, sem):
    low, _, _ = slots_of(order_ref)
    kv_at = 2 * heads * TOK
    stats = stat_rows(x_ref, kv_at + 2 * TOK)

    def store(which, number):
        part = pl.ds(which * 4, 4)
        return copy_of(dkv.at[:, part], local_hbm.at[:, part], sem.at[number])

    local_tiles(
        low, x_ref, stats, heads, x_ref, kv_at, dq_out, dkv, lambda high: store(high, 1).start()
    )
    store(low, 2).start()
    store(1 - low, 1).wait()
    store(low, 2).wait()


def cross0_kernel(heads, order_ref, x_ref, kp_ref, dq_in, msg_hbm, cross_hbm, dq, dkv, out, sem):
    low, prev_low, lower_sees = slots_of(order_ref)
    stats = stat_rows(x_ref, (2 * heads + 2) * TOK)
    cross_tiles(low, prev_low, lower_sees, x_ref, stats, heads, kp_ref, dq, dkv)
    store = copy_of(dkv, cross_hbm, sem.at[0])
    store.start()
    for j in range(heads):
        out[:, j * TOK : (j + 1) * TOK, :] = (dq[j] + dq_in[j]).astype(BF)
    send = send_rows(out, msg_hbm, 0, sem.at[1])
    store.wait()
    send.wait()


def cross1_kernel(heads, order_ref, x_ref, kp_ref, cross_hbm, dq_hbm, cross_out, dq, dkv, held, sem):
    low, prev_low, lower_sees = slots_of(order_ref)
    held_load = copy_of(cross_hbm, held, sem.at[1])
    held_load.start()
    stats = stat_rows(x_ref, 2 * heads * TOK)
    cross_tiles(low, prev_low, lower_sees, x_ref, stats, heads, kp_ref, dq, dkv)
    store = copy_of(dq, dq_hbm, sem.at[2])
    store.start()
    held_load.wait()
    cross_out[...] = (dkv[...] + held[...]).astype(BF)
    store.wait()


def local1_kernel(
    heads, kv_at, order_ref, x_ref, x0_ref, dq_hbm, local_hbm, msg_in, msg_hbm, local_out,
    dq, dq_held, held, out, sem,
):
    del msg_in
    low, _, _ = slots_of(order_ref)
    dq_load = copy_of(dq_hbm, dq_held, sem.at[2])
    held_load = copy_of(local_hbm, held, sem.at[3])
    dq_load.start()
    held_load.start()
    stats = stat_rows(x_ref, 2 * heads * TOK)
    local_tiles(low, x_ref, stats, heads, x0_ref, kv_at, dq, local_out, lambda high: None)
    dq_load.wait()
    for j in range(heads):
        out[:, j * TOK : (j + 1) * TOK, :] = (dq[j] + dq_held[j]).astype(BF)
    send = send_rows(out, msg_hbm, heads * TOK, sem.at[4])
    held_load.wait()
    local_out[...] += held[...]
    send.wait()


def add_kernel(heads, local_ref, back_ref, msg_in, msg_hbm, out, sem):
    del msg_in
    for i in range(2):
        total = local_ref[i] + back_ref[i].astype(F32)
        out[:, i * TOK : (i + 1) * TOK, :] = total.astype(BF)
    send_rows(out, msg_hbm, 2 * heads * TOK, sem.at[0]).wait()


def unpack_kernel(x_hbm, dq_ref, dk_ref, dv_ref, buf, in_sem, sem):
    loads = [copy_of(x_hbm.at[u], buf.at[u], in_sem.at[u]) for u in range(N_ULY)]
    for load in loads:
        load.start()

    def store(u, at, target, column, which):
        cols = pl.ds(pl.multiple_of(column * D, D), D)
        copy_of(buf.at[u, pl.ds(at, TOK), :], target.at[:, cols], sem.at[which]).start()

    for u in range(N_ULY):
        group = head_group(device_at(u))
        loads[u].wait()
        for j in range(GROUP):
            store(u, j * TOK, dq_ref, group * GROUP + j, 0)
        store(u, GROUP * TOK, dk_ref, group, 1)
        store(u, (GROUP + 1) * TOK, dv_ref, group, 2)
    for which, ref in enumerate((dq_ref, dk_ref, dv_ref)):
        copy_of(ref, ref, sem.at[which]).wait()


def params():
    return pltpu.CompilerParams(vmem_limit_bytes=32 * MIB)


def shift_slot(value, by):
    pairs = []
    for slot in range(16):
        other = (slot + by) % 16
        flip = 1 if slot // 8 != other // 8 else 0
        pairs += [(slot * N_ULY + u, other * N_ULY + (u ^ flip)) for u in range(N_ULY)]
    return lax.ppermute(value, ("blk", "uly"), pairs)


def exchange(value):
    groups = [[b * N_ULY + u for u in ORDERS[b % 2]] for b in range(16)]
    return lax.all_to_all(
        value, ("blk", "uly"), split_axis=0, concat_axis=0, axis_index_groups=groups, tiled=True
    )


def call(kernel, inputs, outs, scratch, units, name, aliases=None):
    def placed(array, space):
        return pltpu.with_memory_space_constraint(array, space) if space == pltpu.HBM else array

    def shaped(shape, space):
        return pltpu.HBM(*shape) if space == pltpu.HBM else jax.ShapeDtypeStruct(*shape)

    return pl.pallas_call(
        kernel,
        in_specs=[pl.BlockSpec(memory_space=space) for _, space in inputs],
        out_specs=[pl.BlockSpec(memory_space=space) for _, space in outs],
        out_shape=[shaped(shape, space) for shape, space in outs],
        scratch_shapes=scratch,
        input_output_aliases=aliases or {},
        compiler_params=params(),
        cost_estimate=pl.CostEstimate(
            flops=units * 5 * 2 * 512 * 512 * 128 * 2,
            bytes_accessed=4 * MIB,
            transcendentals=units * 512 * 512,
        ),
        name=name,
    )(*[placed(array, space) for array, space in inputs])


def body(queries, input_keys, input_values, outputs, output_gradient, saved_logsumexp, span_order):
    h = 2
    kv_at = 2 * h * TOK
    rows4 = (N_ULY, TOK, D)
    lse = saved_logsumexp.T
    order = (span_order.T, pltpu.SMEM)
    msg0 = pack(queries, output_gradient, outputs, lse, (input_keys, input_values), 0, h)
    x0 = exchange(msg0)
    msg1 = pack(queries, output_gradient, outputs, lse, (), h, h)
    x0, msg1 = lax.optimization_barrier((x0, msg1))
    x1 = exchange(msg1)
    kv_prev = shift_slot(x0[:, kv_at : kv_at + 2 * TOK, :], 1)

    vmem, hbm = pltpu.VMEM, pltpu.HBM
    head_sums = ((h,) + rows4, F32)
    pair_sums = ((2,) + rows4, F32)
    pair_low = ((2,) + rows4, BF)
    head_low = ((N_ULY, h * TOK, D), BF)
    message = ((N_ULY, (GROUP + 2) * TOK, D), BF)
    sems = pltpu.SemaphoreType.DMA((5,))
    dq0, local = call(
        functools.partial(local0_kernel, h),
        (order, (x0, vmem)),
        ((head_sums, vmem), (pair_sums, hbm)),
        [pltpu.VMEM(*pair_sums), sems],
        3 * h,
        "local_first",
    )
    msg, cross = call(
        functools.partial(cross0_kernel, h),
        (order, (x0, vmem), (kv_prev, vmem), (dq0, vmem)),
        ((message, hbm), (pair_sums, hbm)),
        [pltpu.VMEM(*head_sums), pltpu.VMEM(*pair_sums), pltpu.VMEM(*head_low), sems],
        2 * h,
        "cross_first",
    )
    dq1, cross_low = call(
        functools.partial(cross1_kernel, h),
        (order, (x1, vmem), (kv_prev, vmem), (cross, hbm)),
        ((head_sums, hbm), (pair_low, vmem)),
        [
            pltpu.VMEM(*head_sums),
            pltpu.VMEM(*pair_sums),
            pltpu.VMEM(*pair_sums),
            sems,
        ],
        2 * h,
        "cross_last",
    )
    back = shift_slot(cross_low, -1)
    msg, local = call(
        functools.partial(local1_kernel, h, kv_at),
        (order, (x1, vmem), (x0, vmem), (dq1, hbm), (local, hbm), (msg, hbm)),
        ((message, hbm), (pair_sums, vmem)),
        [
            pltpu.VMEM(*head_sums),
            pltpu.VMEM(*head_sums),
            pltpu.VMEM(*pair_sums),
            pltpu.VMEM(*head_low),
            sems,
        ],
        3 * h,
        "local_last",
        {5: 0},
    )
    (msg,) = call(
        functools.partial(add_kernel, h),
        ((local, vmem), (back, vmem), (msg, hbm)),
        ((message, hbm),),
        [pltpu.VMEM((N_ULY, 2 * TOK, D), BF), sems],
        0,
        "add_returned",
        {2: 0},
    )
    result = exchange(msg)
    return call(
        unpack_kernel,
        ((result, hbm),),
        (
            (((TOK, N_ULY * GROUP * D), BF), hbm),
            (((TOK, N_ULY * D), BF), hbm),
            (((TOK, N_ULY * D), BF), hbm),
        ),
        [
            pltpu.VMEM(*message),
            pltpu.SemaphoreType.DMA((N_ULY,)),
            pltpu.SemaphoreType.DMA((3,)),
        ],
        0,
        "unpack",
    )


def solution(mesh):
    rows = P(("blk", "uly"), None)
    return jax.shard_map(
        body, mesh=mesh, in_specs=(rows,) * 6 + (P(),), out_specs=(rows,) * 3, check_vma=False
    )
```

```python
import functools
import math

import jax
import jax.numpy as jnp
from jax import lax
from jax.experimental import pallas as pl
from jax.experimental.pallas import tpu as pltpu
from jax.sharding import PartitionSpec as P

D = 128
N_ULY = 8
TOK = 128
GROUP = 4
HALF = 512
FACTOR = 1.0 / math.sqrt(D)
LOG2E = math.log2(math.e)
STAT = 16
BF = jnp.bfloat16
F32 = jnp.float32
MIB = 1 << 20
ORDERS = ((0, 2, 4, 6, 1, 3, 5, 7), (7, 6, 5, 4, 3, 2, 1, 0))
PLACES = tuple(tuple(order.index(u) for u in range(N_ULY)) for order in ORDERS)


def parity():
    return lax.axis_index("blk") % 2


def choose(table, index, odd):
    return table[0][index] + odd * (table[1][index] - table[0][index])


def device_at(place):
    return choose(ORDERS, place, parity())


def place_of(u):
    return choose(PLACES, u, parity())


def nt(a, b):
    return lax.dot_general(a, b, (((1,), (1,)), ((), ())), preferred_element_type=F32)


def nn(a, b):
    return jnp.dot(a, b, preferred_element_type=F32)


def tn(a, b):
    return lax.dot_general(a, b, (((0,), (0,)), ((), ())), preferred_element_type=F32)


def copy_of(source, target, sem):
    return pltpu.make_async_copy(source, target, sem)


def head_group(u):
    upper = lax.axis_index("blk") // 8
    return u ^ upper


def pack_kernel(first, heads, with_kv, *refs):
    if with_kv:
        q_ref, do_ref, o_ref, lse_hbm, k_ref, v_ref, msg_ref, buf, o_buf, lse_ref, sem = refs
    else:
        q_ref, do_ref, o_ref, lse_hbm, msg_ref, buf, o_buf, lse_ref, sem = refs
    rows = 2 * heads * TOK + (2 * TOK if with_kv else 0)
    lse_load = copy_of(lse_hbm, lse_ref, sem.at[3, 0])
    lse_load.start()

    groups = [head_group(device_at(i)) for i in range(N_ULY)]
    for u, group in enumerate(groups):

        def load(source, column, at):
            cols = pl.ds(pl.multiple_of(column * D, D), D)
            copy_of(source.at[:, cols], buf.at[u, pl.ds(at, TOK), :], sem.at[0, u]).start()

        o_cols = pl.ds(pl.multiple_of((group * GROUP + first) * D, D), heads * D)
        copy_of(o_ref.at[:, o_cols], o_buf.at[u], sem.at[1, u]).start()
        for j in range(heads):
            load(do_ref, group * GROUP + first + j, (heads + j) * TOK)
        for j in range(heads):
            load(q_ref, group * GROUP + first + j, j * TOK)
        if with_kv:
            load(k_ref, group, 2 * heads * TOK)
            load(v_ref, group, (2 * heads + 1) * TOK)
    row_of = lax.broadcasted_iota(jnp.int32, (8, D), 0)
    lse_load.wait()
    for u in range(N_ULY):
        loaded = buf.at[u, pl.ds(0, rows), :]
        copy_of(loaded, loaded, sem.at[0, u]).wait()
        copy_of(o_buf.at[u], o_buf.at[u], sem.at[1, u]).wait()
        at = groups[u] * GROUP + first
        stats = jnp.zeros((8, TOK), F32)
        for j in range(heads):
            grads = buf[u, (heads + j) * TOK : (heads + j + 1) * TOK, :].astype(F32)
            product = grads * o_buf[u, :, j * D : (j + 1) * D].astype(F32)
            high = product.astype(BF)
            low = (product - high.astype(F32)).astype(BF)
            ones = jnp.where(row_of == heads + j, 1.0, 0.0).astype(BF)
            stats = stats + nt(ones, high) + nt(ones, low)
            lse_one = lse_ref[pl.ds(at + j, 1), :] * LOG2E
            stats = stats + jnp.where(row_of == j, lse_one, 0.0)
        stats = stats[: 2 * heads]
        p0 = stats.astype(BF).astype(F32)
        p1 = (stats - p0).astype(BF).astype(F32)
        p2 = stats - p0 - p1
        pieces = jnp.concatenate([p0, p1, p2, jnp.zeros_like(p0)], axis=0)
        buf[u, rows : rows + STAT, :] = pieces.astype(BF)
        copy_of(buf.at[u], msg_ref.at[u], sem.at[2, u]).start()
    for u in range(N_ULY):
        copy_of(buf.at[u], msg_ref.at[u], sem.at[2, u]).wait()


def pack(queries, grads, outputs, lse, kv, first, heads):
    rows = 2 * heads * TOK + STAT + (2 * TOK if kv else 0)
    message = ((N_ULY, rows, D), BF)
    (msg,) = call(
        functools.partial(pack_kernel, first, heads, bool(kv)),
        [(array, pltpu.HBM) for array in (queries, grads, outputs, lse) + kv],
        ((message, pltpu.HBM),),
        [
            pltpu.VMEM(*message),
            pltpu.VMEM((N_ULY, TOK, heads * D), BF),
            pltpu.VMEM(lse.shape, F32),
            pltpu.SemaphoreType.DMA((4, N_ULY)),
        ],
        1,
        "pack_heads_%d" % first,
    )
    return msg


def slots_of(order_ref):
    slot = lax.axis_index("blk")
    prev = lax.rem(slot + 15, 16)
    a, b = order_ref[0, slot], order_ref[1, slot]
    pa, pb = order_ref[0, prev], order_ref[1, prev]
    low = (a > b).astype(jnp.int32)
    prev_low = (pa > pb).astype(jnp.int32)
    lower_sees = jnp.minimum(a, b) > jnp.minimum(pa, pb)
    return low, prev_low, lower_sees


def half(ref, which, at, odd=None):
    odd = parity() if odd is None else odd
    parts = []
    for b in range(4):
        lower, upper = choose(PLACES, b, odd), choose(PLACES, 4 + b, odd)
        parts.append(ref[lower + which * (upper - lower), at : at + TOK, :])
    return jnp.concatenate(parts, axis=0)


def key_grads(rows, k, v, heads=None):
    q, do, lse, delta = rows
    probs = jnp.exp2(nt(k, q) * (FACTOR * LOG2E) - lse)
    if heads is not None:
        key = lax.broadcasted_iota(jnp.int32, probs.shape, 0)
        row = lax.broadcasted_iota(jnp.int32, probs.shape, 1) % (probs.shape[1] // heads)
        probs = jnp.where(row >= key, probs, 0.0)
    d_scores = (probs * (nt(v, do) - delta) * FACTOR).astype(BF)
    return nn(probs.astype(BF), do), nn(d_scores, q), d_scores


def tile(rows, k, v, heads=None):
    dv, dk, d_scores = key_grads(rows, k, v, heads)
    return dv, dk, tn(d_scores, k)


def stat_rows(x_ref, at):
    parts = []
    for s in range(N_ULY):
        p = x_ref[place_of(s), at : at + STAT, :].astype(F32)
        parts.append(p[0:4] + p[4:8] + p[8:12])
    return jnp.concatenate(parts, axis=1)


def pick(stats, row, which):
    lower, upper = stats[row : row + 1, :HALF], stats[row : row + 1, HALF:]
    return jnp.where(which == 0, lower, upper)


def rows_of(x_ref, stats, heads, which):
    def join(at):
        return jnp.concatenate([half(x_ref, which, (at + j) * TOK) for j in range(heads)], axis=0)

    def join_stats(at):
        return jnp.concatenate([pick(stats, at + j, which) for j in range(heads)], axis=1)

    return join(0), join(heads), join_stats(0), join_stats(heads)


def upper_rows(rows, heads):
    q, do, lse, delta = rows
    q, do = [
        jnp.concatenate([a[j * HALF + 256 : (j + 1) * HALF] for j in range(heads)], 0)
        for a in (q, do)
    ]
    lse, delta = [
        jnp.concatenate([a[:, j * HALF + 256 : (j + 1) * HALF] for j in range(heads)], 1)
        for a in (lse, delta)
    ]
    return q, do, lse, delta


def diagonal(rows, k, v, heads):
    dv0, dk0, dq0 = tile(rows, k[:256], v[:256], heads)
    dv1, dk1, dq1 = tile(upper_rows(rows, heads), k[256:], v[256:], heads)
    dq = []
    for j in range(heads):
        at = j * HALF
        dq.append(dq0[at : at + 256])
        dq.append(dq0[at + 256 : at + HALF] + dq1[j * 256 : (j + 1) * 256])
    return (
        jnp.concatenate([dv0, dv1], 0),
        jnp.concatenate([dk0, dk1], 0),
        jnp.concatenate(dq, 0),
    )


def blocks(value):
    return value.reshape(4, TOK, D)


def put(ref, index, which, value, add=False):
    at = (index, pl.ds(which * 4, 4))
    ref[at] = ref[at] + blocks(value) if add else blocks(value)


def put_heads(ref, heads, which, value, add=False):
    for j in range(heads):
        put(ref, j, which, value[j * HALF : (j + 1) * HALF], add)


def local_tiles(low, x_ref, stats, heads, k_ref, k_at, dq, dkv, after_high):
    high = 1 - low
    k_low, v_low = half(k_ref, low, k_at), half(k_ref, low, k_at + TOK)
    k_high, v_high = half(k_ref, high, k_at), half(k_ref, high, k_at + TOK)
    rows_high = rows_of(x_ref, stats, heads, high)
    rows_low = rows_of(x_ref, stats, heads, low)
    dv2, dk2, dq2 = diagonal(rows_high, k_high, v_high, heads)
    put(dkv, 0, high, dk2)
    put(dkv, 1, high, dv2)
    after_high(high)
    dv, dk, dq1 = tile(rows_high, k_low, v_low)
    put_heads(dq, heads, high, dq1 + dq2)
    dv3, dk3, dq3 = diagonal(rows_low, k_low, v_low, heads)
    put(dkv, 0, low, dk + dk3)
    put(dkv, 1, low, dv + dv3)
    put_heads(dq, heads, low, dq3)


def second_tile(low, prev_low, lower_sees):
    sees = lower_sees.astype(jnp.int32)
    return sees * low + (1 - sees) * (1 - low), sees * prev_low + (1 - sees) * (1 - prev_low)


def cross_tiles(low, prev_low, lower_sees, x_ref, stats, heads, kp_ref, dkv, first, second):
    odd = 1 - parity()

    def one(rows_at, keys_at, take, add):
        k, v = half(kp_ref, keys_at, 0, odd), half(kp_ref, keys_at, TOK, odd)
        dv, dk, d_scores = key_grads(rows_of(x_ref, stats, heads, rows_at), k, v)
        put(dkv, 0, keys_at, dk, add)
        put(dkv, 1, keys_at, dv, add)
        take(rows_at, k, d_scores)

    one(1 - low, prev_low, first, False)
    dkv[:, pl.ds((1 - prev_low) * 4, 4)] = jnp.zeros((2, 4, TOK, D), F32)
    one(*second_tile(low, prev_low, lower_sees), second, True)


def send_rows(out, msg_hbm, at, sem):
    rows = out.shape[1]
    for u in range(N_ULY):
        copy_of(out.at[u], msg_hbm.at[place_of(u), pl.ds(at, rows), :], sem).start()
    return copy_of(out, out, sem)


def local0_kernel(heads, order_ref, x_ref, dq_out, local_hbm, dkv, sem):
    low, _, _ = slots_of(order_ref)
    kv_at = 2 * heads * TOK
    stats = stat_rows(x_ref, kv_at + 2 * TOK)

    def store(which, number):
        part = pl.ds(which * 4, 4)
        return copy_of(dkv.at[:, part], local_hbm.at[:, part], sem.at[number])

    local_tiles(
        low, x_ref, stats, heads, x_ref, kv_at, dq_out, dkv, lambda high: store(high, 1).start()
    )
    store(low, 2).start()
    store(1 - low, 1).wait()
    store(low, 2).wait()


def cross0_kernel(heads, order_ref, x_ref, kp_ref, dq_in, msg_hbm, cross_hbm, dq, dkv, out, sem):
    low, prev_low, lower_sees = slots_of(order_ref)
    stats = stat_rows(x_ref, (2 * heads + 2) * TOK)

    def first(rows_at, k, d_scores):
        put_heads(dq, heads, rows_at, tn(d_scores, k))
        dq[:, pl.ds(low * 4, 4)] = jnp.zeros((heads, 4, TOK, D), F32)

    def second(rows_at, k, d_scores):
        put_heads(dq, heads, rows_at, tn(d_scores, k), True)

    cross_tiles(low, prev_low, lower_sees, x_ref, stats, heads, kp_ref, dkv, first, second)
    store = copy_of(dkv, cross_hbm, sem.at[0])
    store.start()
    for j in range(heads):
        out[:, j * TOK : (j + 1) * TOK, :] = (dq[j] + dq_in[j]).astype(BF)
    send = send_rows(out, msg_hbm, 0, sem.at[1])
    store.wait()
    send.wait()


def cross1_kernel(heads, order_ref, x_ref, kp_ref, cross_hbm, ds_out, cross_out, dkv, held, sem):
    low, prev_low, lower_sees = slots_of(order_ref)
    held_load = copy_of(cross_hbm, held, sem.at[1])
    held_load.start()
    stats = stat_rows(x_ref, 2 * heads * TOK)

    def keep(number):
        def take(rows_at, k, d_scores):
            ds_out[number] = d_scores

        return take

    cross_tiles(low, prev_low, lower_sees, x_ref, stats, heads, kp_ref, dkv, keep(0), keep(1))
    held_load.wait()
    cross_out[...] = (dkv[...] + held[...]).astype(BF)


def local1_kernel(
    heads, kv_at, order_ref, x_ref, x0_ref, kp_ref, ds_ref, local_hbm, msg_in, msg_hbm, local_out,
    dq, held, out, sem,
):
    del msg_in
    low, prev_low, lower_sees = slots_of(order_ref)
    held_load = copy_of(local_hbm, held, sem.at[3])
    held_load.start()
    stats = stat_rows(x_ref, 2 * heads * TOK)
    local_tiles(low, x_ref, stats, heads, x0_ref, kv_at, dq, local_out, lambda high: None)
    odd = 1 - parity()
    tiles = ((1 - low, prev_low), second_tile(low, prev_low, lower_sees))
    for number, (rows_at, keys_at) in enumerate(tiles):
        k = half(kp_ref, keys_at, 0, odd)
        put_heads(dq, heads, rows_at, tn(ds_ref[number], k), True)
    for j in range(heads):
        out[:, j * TOK : (j + 1) * TOK, :] = dq[j].astype(BF)
    send = send_rows(out, msg_hbm, heads * TOK, sem.at[4])
    held_load.wait()
    local_out[...] += held[...]
    send.wait()


def add_kernel(heads, local_ref, back_ref, msg_in, msg_hbm, out, sem):
    del msg_in
    sends = []
    for u in range(N_ULY):
        for i in range(2):
            total = local_ref[i, u] + back_ref[i, u].astype(F32)
            out[u, i * TOK : (i + 1) * TOK, :] = total.astype(BF)
        rows = pl.ds(2 * heads * TOK, 2 * TOK)
        sends.append(copy_of(out.at[u], msg_hbm.at[place_of(u), rows, :], sem.at[u]))
        sends[u].start()
    for send in sends:
        send.wait()


def unpack_kernel(x_ref, dq_ref, dk_ref, dv_ref, sem):
    def store(u, at, target, column, which):
        cols = pl.ds(pl.multiple_of(column * D, D), D)
        copy_of(x_ref.at[u, pl.ds(at, TOK), :], target.at[:, cols], sem.at[which]).start()

    for u in range(N_ULY):
        group = head_group(device_at(u))
        for j in range(GROUP):
            store(u, j * TOK, dq_ref, group * GROUP + j, 0)
        store(u, GROUP * TOK, dk_ref, group, 1)
        store(u, (GROUP + 1) * TOK, dv_ref, group, 2)
    for which, ref in enumerate((dq_ref, dk_ref, dv_ref)):
        copy_of(ref, ref, sem.at[which]).wait()


def params():
    return pltpu.CompilerParams(vmem_limit_bytes=32 * MIB)


def shift_slot(value, by):
    pairs = []
    for slot in range(16):
        other = (slot + by) % 16
        flip = 1 if slot // 8 != other // 8 else 0
        pairs += [(slot * N_ULY + u, other * N_ULY + (u ^ flip)) for u in range(N_ULY)]
    return lax.ppermute(value, ("blk", "uly"), pairs)


def exchange(value):
    groups = [[b * N_ULY + u for u in ORDERS[b % 2]] for b in range(16)]
    return lax.all_to_all(
        value, ("blk", "uly"), split_axis=0, concat_axis=0, axis_index_groups=groups, tiled=True
    )


def call(kernel, inputs, outs, scratch, units, name, aliases=None):
    def placed(array, space):
        return pltpu.with_memory_space_constraint(array, space) if space == pltpu.HBM else array

    def shaped(shape, space):
        return pltpu.HBM(*shape) if space == pltpu.HBM else jax.ShapeDtypeStruct(*shape)

    return pl.pallas_call(
        kernel,
        in_specs=[pl.BlockSpec(memory_space=space) for _, space in inputs],
        out_specs=[pl.BlockSpec(memory_space=space) for _, space in outs],
        out_shape=[shaped(shape, space) for shape, space in outs],
        scratch_shapes=scratch,
        input_output_aliases=aliases or {},
        compiler_params=params(),
        cost_estimate=pl.CostEstimate(
            flops=units * 5 * 2 * 512 * 512 * 128 * 2,
            bytes_accessed=4 * MIB,
            transcendentals=units * 512 * 512,
        ),
        name=name,
    )(*[placed(array, space) for array, space in inputs])


def body(queries, input_keys, input_values, outputs, output_gradient, saved_logsumexp, span_order):
    h = 2
    kv_at = 2 * h * TOK
    rows4 = (N_ULY, TOK, D)
    lse = saved_logsumexp.T
    order = (span_order.T, pltpu.SMEM)
    msg0 = pack(queries, output_gradient, outputs, lse, (input_keys, input_values), 0, h)
    x0 = exchange(msg0)
    msg1 = pack(queries, output_gradient, outputs, lse, (), h, h)
    x0, msg1 = lax.optimization_barrier((x0, msg1))
    x1 = exchange(msg1)
    kv_prev = shift_slot(x0[:, kv_at : kv_at + 2 * TOK, :], 1)

    vmem, hbm = pltpu.VMEM, pltpu.HBM
    head_sums = ((h,) + rows4, F32)
    pair_sums = ((2,) + rows4, F32)
    pair_low = ((2,) + rows4, BF)
    head_low = ((N_ULY, h * TOK, D), BF)
    message = ((N_ULY, (GROUP + 2) * TOK, D), BF)
    sems = pltpu.SemaphoreType.DMA((N_ULY,))
    dq0, local = call(
        functools.partial(local0_kernel, h),
        (order, (x0, vmem)),
        ((head_sums, vmem), (pair_sums, hbm)),
        [pltpu.VMEM(*pair_sums), sems],
        3 * h,
        "local_first",
    )
    msg, cross = call(
        functools.partial(cross0_kernel, h),
        (order, (x0, vmem), (kv_prev, vmem), (dq0, vmem)),
        ((message, hbm), (pair_sums, hbm)),
        [pltpu.VMEM(*head_sums), pltpu.VMEM(*pair_sums), pltpu.VMEM(*head_low), sems],
        2 * h,
        "cross_first",
    )
    d_scores, cross_low = call(
        functools.partial(cross1_kernel, h),
        (order, (x1, vmem), (kv_prev, vmem), (cross, hbm)),
        ((((2, HALF, h * HALF), BF), vmem), (pair_low, vmem)),
        [pltpu.VMEM(*pair_sums), pltpu.VMEM(*pair_sums), sems],
        2 * h,
        "cross_last",
    )
    back = shift_slot(cross_low, -1)
    msg, local = call(
        functools.partial(local1_kernel, h, kv_at),
        (
            order, (x1, vmem), (x0, vmem), (kv_prev, vmem), (d_scores, vmem), (local, hbm),
            (msg, hbm),
        ),
        ((message, hbm), (pair_sums, vmem)),
        [pltpu.VMEM(*head_sums), pltpu.VMEM(*pair_sums), pltpu.VMEM(*head_low), sems],
        3 * h,
        "local_last",
        {6: 0},
    )
    (msg,) = call(
        functools.partial(add_kernel, h),
        ((local, vmem), (back, vmem), (msg, hbm)),
        ((message, hbm),),
        [pltpu.VMEM((N_ULY, 2 * TOK, D), BF), sems],
        0,
        "add_returned",
        {2: 0},
    )
    result = exchange(msg)
    return call(
        unpack_kernel,
        ((result, vmem),),
        (
            (((TOK, N_ULY * GROUP * D), BF), hbm),
            (((TOK, N_ULY * D), BF), hbm),
            (((TOK, N_ULY * D), BF), hbm),
        ),
        [
            pltpu.SemaphoreType.DMA((3,)),
        ],
        0,
        "unpack",
    )


def solution(mesh):
    rows = P(("blk", "uly"), None)
    return jax.shard_map(
        body, mesh=mesh, in_specs=(rows,) * 6 + (P(),), out_specs=(rows,) * 3, check_vma=False
    )
```

```python
import functools
import math

import jax
import jax.numpy as jnp
from jax import lax
from jax.experimental import pallas as pl
from jax.experimental.pallas import tpu as pltpu
from jax.sharding import PartitionSpec as P

D = 128
N_ULY = 8
TOK = 128
GROUP = 4
HALF = 512
FACTOR = 1.0 / math.sqrt(D)
LOG2E = math.log2(math.e)
STAT = 16
BF = jnp.bfloat16
F32 = jnp.float32
MIB = 1 << 20
ORDERS = ((0, 2, 4, 6, 1, 3, 5, 7), (7, 4, 3, 0, 6, 5, 2, 1))
PLACES = tuple(tuple(order.index(u) for u in range(N_ULY)) for order in ORDERS)


def parity():
    return lax.axis_index("blk") % 2


def choose(table, index, odd):
    return table[0][index] + odd * (table[1][index] - table[0][index])


def device_at(place):
    return choose(ORDERS, place, parity())


def place_of(u):
    return choose(PLACES, u, parity())


def nt(a, b):
    return lax.dot_general(a, b, (((1,), (1,)), ((), ())), preferred_element_type=F32)


def nn(a, b):
    return jnp.dot(a, b, preferred_element_type=F32)


def tn(a, b):
    return lax.dot_general(a, b, (((0,), (0,)), ((), ())), preferred_element_type=F32)


def copy_of(source, target, sem):
    return pltpu.make_async_copy(source, target, sem)


def head_group(u):
    upper = lax.axis_index("blk") // 8
    return u ^ upper


def pack_kernel(first, heads, with_kv, *refs):
    if with_kv:
        q_ref, do_ref, o_ref, lse_hbm, k_ref, v_ref, msg_ref, buf, o_buf, lse_ref, sem = refs
    else:
        q_ref, do_ref, o_ref, lse_hbm, msg_ref, buf, o_buf, lse_ref, sem = refs
    rows = 2 * heads * TOK + (2 * TOK if with_kv else 0)
    lse_load = copy_of(lse_hbm, lse_ref, sem.at[3, 0])
    lse_load.start()

    groups = [head_group(device_at(i)) for i in range(N_ULY)]
    for u, group in enumerate(groups):

        def load(source, column, at):
            cols = pl.ds(pl.multiple_of(column * D, D), D)
            copy_of(source.at[:, cols], buf.at[u, pl.ds(at, TOK), :], sem.at[0, u]).start()

        o_cols = pl.ds(pl.multiple_of((group * GROUP + first) * D, D), heads * D)
        copy_of(o_ref.at[:, o_cols], o_buf.at[u], sem.at[1, u]).start()
        for j in range(heads):
            load(do_ref, group * GROUP + first + j, (heads + j) * TOK)
        for j in range(heads):
            load(q_ref, group * GROUP + first + j, j * TOK)
        if with_kv:
            load(k_ref, group, 2 * heads * TOK)
            load(v_ref, group, (2 * heads + 1) * TOK)
    row_of = lax.broadcasted_iota(jnp.int32, (8, D), 0)
    lse_load.wait()
    for u in range(N_ULY):
        loaded = buf.at[u, pl.ds(0, rows), :]
        copy_of(loaded, loaded, sem.at[0, u]).wait()
        copy_of(o_buf.at[u], o_buf.at[u], sem.at[1, u]).wait()
        at = groups[u] * GROUP + first
        stats = jnp.zeros((8, TOK), F32)
        for j in range(heads):
            grads = buf[u, (heads + j) * TOK : (heads + j + 1) * TOK, :].astype(F32)
            product = grads * o_buf[u, :, j * D : (j + 1) * D].astype(F32)
            high = product.astype(BF)
            low = (product - high.astype(F32)).astype(BF)
            ones = jnp.where(row_of == heads + j, 1.0, 0.0).astype(BF)
            stats = stats + nt(ones, high) + nt(ones, low)
            lse_one = lse_ref[pl.ds(at + j, 1), :] * LOG2E
            stats = stats + jnp.where(row_of == j, lse_one, 0.0)
        stats = stats[: 2 * heads]
        p0 = stats.astype(BF).astype(F32)
        p1 = (stats - p0).astype(BF).astype(F32)
        p2 = stats - p0 - p1
        pieces = jnp.concatenate([p0, p1, p2, jnp.zeros_like(p0)], axis=0)
        buf[u, rows : rows + STAT, :] = pieces.astype(BF)
        copy_of(buf.at[u], msg_ref.at[u], sem.at[2, u]).start()
    for u in range(N_ULY):
        copy_of(buf.at[u], msg_ref.at[u], sem.at[2, u]).wait()


def pack(queries, grads, outputs, lse, kv, first, heads):
    rows = 2 * heads * TOK + STAT + (2 * TOK if kv else 0)
    message = ((N_ULY, rows, D), BF)
    (msg,) = call(
        functools.partial(pack_kernel, first, heads, bool(kv)),
        [(array, pltpu.HBM) for array in (queries, grads, outputs, lse) + kv],
        ((message, pltpu.HBM),),
        [
            pltpu.VMEM(*message),
            pltpu.VMEM((N_ULY, TOK, heads * D), BF),
            pltpu.VMEM(lse.shape, F32),
            pltpu.SemaphoreType.DMA((4, N_ULY)),
        ],
        1,
        "pack_heads_%d" % first,
    )
    return msg


def slots_of(order_ref):
    slot = lax.axis_index("blk")
    prev = lax.rem(slot + 15, 16)
    a, b = order_ref[0, slot], order_ref[1, slot]
    pa, pb = order_ref[0, prev], order_ref[1, prev]
    low = (a > b).astype(jnp.int32)
    prev_low = (pa > pb).astype(jnp.int32)
    lower_sees = jnp.minimum(a, b) > jnp.minimum(pa, pb)
    return low, prev_low, lower_sees


def half(ref, which, at, odd=None):
    odd = parity() if odd is None else odd
    parts = []
    for b in range(4):
        lower, upper = choose(PLACES, b, odd), choose(PLACES, 4 + b, odd)
        parts.append(ref[lower + which * (upper - lower), at : at + TOK, :])
    return jnp.concatenate(parts, axis=0)


def key_grads(rows, k, v, heads=None):
    q, do, lse, delta = rows
    probs = jnp.exp2(nt(k, q) * (FACTOR * LOG2E) - lse)
    if heads is not None:
        key = lax.broadcasted_iota(jnp.int32, probs.shape, 0)
        row = lax.broadcasted_iota(jnp.int32, probs.shape, 1) % (probs.shape[1] // heads)
        probs = jnp.where(row >= key, probs, 0.0)
    d_scores = (probs * (nt(v, do) - delta) * FACTOR).astype(BF)
    return nn(probs.astype(BF), do), nn(d_scores, q), d_scores


def tile(rows, k, v, heads=None):
    dv, dk, d_scores = key_grads(rows, k, v, heads)
    return dv, dk, tn(d_scores, k)


def stat_rows(x_ref, at):
    parts = []
    for s in range(N_ULY):
        p = x_ref[place_of(s), at : at + STAT, :].astype(F32)
        parts.append(p[0:4] + p[4:8] + p[8:12])
    return jnp.concatenate(parts, axis=1)


def pick(stats, row, which):
    lower, upper = stats[row : row + 1, :HALF], stats[row : row + 1, HALF:]
    return jnp.where(which == 0, lower, upper)


def rows_of(x_ref, stats, heads, which):
    def join(at):
        return jnp.concatenate([half(x_ref, which, (at + j) * TOK) for j in range(heads)], axis=0)

    def join_stats(at):
        return jnp.concatenate([pick(stats, at + j, which) for j in range(heads)], axis=1)

    return join(0), join(heads), join_stats(0), join_stats(heads)


def upper_rows(rows, heads):
    q, do, lse, delta = rows
    q, do = [
        jnp.concatenate([a[j * HALF + 256 : (j + 1) * HALF] for j in range(heads)], 0)
        for a in (q, do)
    ]
    lse, delta = [
        jnp.concatenate([a[:, j * HALF + 256 : (j + 1) * HALF] for j in range(heads)], 1)
        for a in (lse, delta)
    ]
    return q, do, lse, delta


def diagonal(rows, k, v, heads):
    dv0, dk0, dq0 = tile(rows, k[:256], v[:256], heads)
    dv1, dk1, dq1 = tile(upper_rows(rows, heads), k[256:], v[256:], heads)
    dq = []
    for j in range(heads):
        at = j * HALF
        dq.append(dq0[at : at + 256])
        dq.append(dq0[at + 256 : at + HALF] + dq1[j * 256 : (j + 1) * 256])
    return (
        jnp.concatenate([dv0, dv1], 0),
        jnp.concatenate([dk0, dk1], 0),
        jnp.concatenate(dq, 0),
    )


def blocks(value):
    return value.reshape(4, TOK, D)


def put(ref, index, which, value, add=False):
    at = (index, pl.ds(which * 4, 4))
    ref[at] = ref[at] + blocks(value) if add else blocks(value)


def put_heads(ref, heads, which, value, add=False):
    for j in range(heads):
        put(ref, j, which, value[j * HALF : (j + 1) * HALF], add)


def local_tiles(low, x_ref, stats, heads, k_ref, k_at, dq, dkv, after_high):
    high = 1 - low
    k_low, v_low = half(k_ref, low, k_at), half(k_ref, low, k_at + TOK)
    k_high, v_high = half(k_ref, high, k_at), half(k_ref, high, k_at + TOK)
    rows_high = rows_of(x_ref, stats, heads, high)
    rows_low = rows_of(x_ref, stats, heads, low)
    dv2, dk2, dq2 = diagonal(rows_high, k_high, v_high, heads)
    put(dkv, 0, high, dk2)
    put(dkv, 1, high, dv2)
    after_high(high)
    dv, dk, dq1 = tile(rows_high, k_low, v_low)
    put_heads(dq, heads, high, dq1 + dq2)
    dv3, dk3, dq3 = diagonal(rows_low, k_low, v_low, heads)
    put(dkv, 0, low, dk + dk3)
    put(dkv, 1, low, dv + dv3)
    put_heads(dq, heads, low, dq3)


def second_tile(low, prev_low, lower_sees):
    sees = lower_sees.astype(jnp.int32)
    return sees * low + (1 - sees) * (1 - low), sees * prev_low + (1 - sees) * (1 - prev_low)


def cross_tiles(low, prev_low, lower_sees, x_ref, stats, heads, kp_ref, dkv, first, second):
    odd = 1 - parity()

    def one(rows_at, keys_at, take, add):
        k, v = half(kp_ref, keys_at, 0, odd), half(kp_ref, keys_at, TOK, odd)
        dv, dk, d_scores = key_grads(rows_of(x_ref, stats, heads, rows_at), k, v)
        put(dkv, 0, keys_at, dk, add)
        put(dkv, 1, keys_at, dv, add)
        take(rows_at, k, d_scores)

    one(1 - low, prev_low, first, False)
    dkv[:, pl.ds((1 - prev_low) * 4, 4)] = jnp.zeros((2, 4, TOK, D), F32)
    one(*second_tile(low, prev_low, lower_sees), second, True)


def send_rows(out, msg_hbm, at, sem):
    rows = out.shape[1]
    for u in range(N_ULY):
        copy_of(out.at[u], msg_hbm.at[place_of(u), pl.ds(at, rows), :], sem).start()
    return copy_of(out, out, sem)


def local0_kernel(heads, order_ref, x_ref, dq_out, local_hbm, dkv, sem):
    low, _, _ = slots_of(order_ref)
    kv_at = 2 * heads * TOK
    stats = stat_rows(x_ref, kv_at + 2 * TOK)

    def store(which, number):
        part = pl.ds(which * 4, 4)
        return copy_of(dkv.at[:, part], local_hbm.at[:, part], sem.at[number])

    local_tiles(
        low, x_ref, stats, heads, x_ref, kv_at, dq_out, dkv, lambda high: store(high, 1).start()
    )
    store(low, 2).start()
    store(1 - low, 1).wait()
    store(low, 2).wait()


def cross0_kernel(heads, order_ref, x_ref, kp_ref, dq_in, msg_hbm, cross_hbm, dq, dkv, out, sem):
    low, prev_low, lower_sees = slots_of(order_ref)
    stats = stat_rows(x_ref, (2 * heads + 2) * TOK)

    def first(rows_at, k, d_scores):
        put_heads(dq, heads, rows_at, tn(d_scores, k))
        dq[:, pl.ds(low * 4, 4)] = jnp.zeros((heads, 4, TOK, D), F32)

    def second(rows_at, k, d_scores):
        put_heads(dq, heads, rows_at, tn(d_scores, k), True)

    cross_tiles(low, prev_low, lower_sees, x_ref, stats, heads, kp_ref, dkv, first, second)
    store = copy_of(dkv, cross_hbm, sem.at[0])
    store.start()
    for j in range(heads):
        out[:, j * TOK : (j + 1) * TOK, :] = (dq[j] + dq_in[j]).astype(BF)
    send = send_rows(out, msg_hbm, 0, sem.at[1])
    store.wait()
    send.wait()


def cross1_kernel(heads, order_ref, x_ref, kp_ref, cross_hbm, ds_out, cross_out, dkv, held, sem):
    low, prev_low, lower_sees = slots_of(order_ref)
    held_load = copy_of(cross_hbm, held, sem.at[1])
    held_load.start()
    stats = stat_rows(x_ref, 2 * heads * TOK)

    def keep(number):
        def take(rows_at, k, d_scores):
            ds_out[number] = d_scores

        return take

    cross_tiles(low, prev_low, lower_sees, x_ref, stats, heads, kp_ref, dkv, keep(0), keep(1))
    held_load.wait()
    cross_out[...] = (dkv[...] + held[...]).astype(BF)


def local1_kernel(
    heads, kv_at, order_ref, x_ref, x0_ref, kp_ref, ds_ref, local_hbm, msg_in, msg_hbm, local_out,
    dq, held, out, sem,
):
    del msg_in
    low, prev_low, lower_sees = slots_of(order_ref)
    held_load = copy_of(local_hbm, held, sem.at[3])
    held_load.start()
    stats = stat_rows(x_ref, 2 * heads * TOK)
    local_tiles(low, x_ref, stats, heads, x0_ref, kv_at, dq, local_out, lambda high: None)
    odd = 1 - parity()
    tiles = ((1 - low, prev_low), second_tile(low, prev_low, lower_sees))
    for number, (rows_at, keys_at) in enumerate(tiles):
        k = half(kp_ref, keys_at, 0, odd)
        put_heads(dq, heads, rows_at, tn(ds_ref[number], k), True)
    for j in range(heads):
        out[:, j * TOK : (j + 1) * TOK, :] = dq[j].astype(BF)
    send = send_rows(out, msg_hbm, heads * TOK, sem.at[4])
    held_load.wait()
    local_out[...] += held[...]
    send.wait()


def add_kernel(heads, local_ref, back_ref, msg_in, msg_hbm, out, sem):
    del msg_in
    sends = []
    for u in range(N_ULY):
        for i in range(2):
            total = local_ref[i, u] + back_ref[i, u].astype(F32)
            out[u, i * TOK : (i + 1) * TOK, :] = total.astype(BF)
        rows = pl.ds(2 * heads * TOK, 2 * TOK)
        sends.append(copy_of(out.at[u], msg_hbm.at[place_of(u), rows, :], sem.at[u]))
        sends[u].start()
    for send in sends:
        send.wait()


def unpack_kernel(x_ref, dq_ref, dk_ref, dv_ref, sem):
    def store(u, at, target, column, which):
        cols = pl.ds(pl.multiple_of(column * D, D), D)
        copy_of(x_ref.at[u, pl.ds(at, TOK), :], target.at[:, cols], sem.at[which]).start()

    for u in range(N_ULY):
        group = head_group(device_at(u))
        for j in range(GROUP):
            store(u, j * TOK, dq_ref, group * GROUP + j, 0)
        store(u, GROUP * TOK, dk_ref, group, 1)
        store(u, (GROUP + 1) * TOK, dv_ref, group, 2)
    for which, ref in enumerate((dq_ref, dk_ref, dv_ref)):
        copy_of(ref, ref, sem.at[which]).wait()


def params():
    return pltpu.CompilerParams(vmem_limit_bytes=32 * MIB)


def shift_slot(value, by):
    pairs = []
    for slot in range(16):
        other = (slot + by) % 16
        flip = 1 if slot // 8 != other // 8 else 0
        pairs += [(slot * N_ULY + u, other * N_ULY + (u ^ flip)) for u in range(N_ULY)]
    return lax.ppermute(value, ("blk", "uly"), pairs)


def exchange(value):
    groups = [[b * N_ULY + u for u in ORDERS[b % 2]] for b in range(16)]
    return lax.all_to_all(
        value, ("blk", "uly"), split_axis=0, concat_axis=0, axis_index_groups=groups, tiled=True
    )


def call(kernel, inputs, outs, scratch, units, name, aliases=None):
    def placed(array, space):
        return pltpu.with_memory_space_constraint(array, space) if space == pltpu.HBM else array

    def shaped(shape, space):
        return pltpu.HBM(*shape) if space == pltpu.HBM else jax.ShapeDtypeStruct(*shape)

    return pl.pallas_call(
        kernel,
        in_specs=[pl.BlockSpec(memory_space=space) for _, space in inputs],
        out_specs=[pl.BlockSpec(memory_space=space) for _, space in outs],
        out_shape=[shaped(shape, space) for shape, space in outs],
        scratch_shapes=scratch,
        input_output_aliases=aliases or {},
        compiler_params=params(),
        cost_estimate=pl.CostEstimate(
            flops=int(units * 5 * 2 * 512 * 512 * 128 * 2),
            bytes_accessed=int(min(units, 4) * MIB),
            transcendentals=int(units * 512 * 512),
        ),
        name=name,
    )(*[placed(array, space) for array, space in inputs])


def body(queries, input_keys, input_values, outputs, output_gradient, saved_logsumexp, span_order):
    h = 2
    kv_at = 2 * h * TOK
    rows4 = (N_ULY, TOK, D)
    lse = saved_logsumexp.T
    order = (span_order.T, pltpu.SMEM)
    msg0 = pack(queries, output_gradient, outputs, lse, (input_keys, input_values), 0, h)
    x0 = exchange(msg0)
    msg1 = pack(queries, output_gradient, outputs, lse, (), h, h)
    x0, msg1 = lax.optimization_barrier((x0, msg1))
    x1 = exchange(msg1)
    kv_prev = shift_slot(x0[:, kv_at : kv_at + 2 * TOK, :], 1)

    vmem, hbm = pltpu.VMEM, pltpu.HBM
    head_sums = ((h,) + rows4, F32)
    pair_sums = ((2,) + rows4, F32)
    pair_low = ((2,) + rows4, BF)
    head_low = ((N_ULY, h * TOK, D), BF)
    message = ((N_ULY, (GROUP + 2) * TOK, D), BF)
    sems = pltpu.SemaphoreType.DMA((N_ULY,))
    dq0, local = call(
        functools.partial(local0_kernel, h),
        (order, (x0, vmem)),
        ((head_sums, vmem), (pair_sums, hbm)),
        [pltpu.VMEM(*pair_sums), sems],
        3 * h,
        "local_first",
    )
    msg, cross = call(
        functools.partial(cross0_kernel, h),
        (order, (x0, vmem), (kv_prev, vmem), (dq0, vmem)),
        ((message, hbm), (pair_sums, hbm)),
        [pltpu.VMEM(*head_sums), pltpu.VMEM(*pair_sums), pltpu.VMEM(*head_low), sems],
        2 * h,
        "cross_first",
    )
    d_scores, cross_low = call(
        functools.partial(cross1_kernel, h),
        (order, (x1, vmem), (kv_prev, vmem), (cross, hbm)),
        ((((2, HALF, h * HALF), BF), vmem), (pair_low, vmem)),
        [pltpu.VMEM(*pair_sums), pltpu.VMEM(*pair_sums), sems],
        2 * h,
        "cross_last",
    )
    back = shift_slot(cross_low, -1)
    msg, local = call(
        functools.partial(local1_kernel, h, kv_at),
        (
            order, (x1, vmem), (x0, vmem), (kv_prev, vmem), (d_scores, vmem), (local, hbm),
            (msg, hbm),
        ),
        ((message, hbm), (pair_sums, vmem)),
        [pltpu.VMEM(*head_sums), pltpu.VMEM(*pair_sums), pltpu.VMEM(*head_low), sems],
        3 * h,
        "local_last",
        {6: 0},
    )
    (msg,) = call(
        functools.partial(add_kernel, h),
        ((local, vmem), (back, vmem), (msg, hbm)),
        ((message, hbm),),
        [pltpu.VMEM((N_ULY, 2 * TOK, D), BF), sems],
        0,
        "add_returned",
        {2: 0},
    )
    result = exchange(msg)
    return call(
        unpack_kernel,
        ((result, vmem),),
        (
            (((TOK, N_ULY * GROUP * D), BF), hbm),
            (((TOK, N_ULY * D), BF), hbm),
            (((TOK, N_ULY * D), BF), hbm),
        ),
        [
            pltpu.SemaphoreType.DMA((3,)),
        ],
        0,
        "unpack",
    )


def solution(mesh):
    rows = P(("blk", "uly"), None)
    return jax.shard_map(
        body, mesh=mesh, in_specs=(rows,) * 6 + (P(),), out_specs=(rows,) * 3, check_vma=False
    )
```

```python
import functools
import math

import jax
import jax.numpy as jnp
from jax import lax
from jax.experimental import pallas as pl
from jax.experimental.pallas import tpu as pltpu
from jax.sharding import PartitionSpec as P

D = 128
N_ULY = 8
TOK = 128
GROUP = 4
HALF = 512
FACTOR = 1.0 / math.sqrt(D)
LOG2E = math.log2(math.e)
STAT = 16
BF = jnp.bfloat16
F32 = jnp.float32
MIB = 1 << 20
ORDERS = ((0, 2, 4, 6, 1, 3, 5, 7), (7, 4, 3, 0, 6, 5, 2, 1))
PLACES = tuple(tuple(order.index(u) for u in range(N_ULY)) for order in ORDERS)


def parity():
    return lax.axis_index("blk") % 2


def choose(table, index, odd):
    return table[0][index] + odd * (table[1][index] - table[0][index])


def device_at(place):
    return choose(ORDERS, place, parity())


def place_of(u):
    return choose(PLACES, u, parity())


def nt(a, b):
    return lax.dot_general(a, b, (((1,), (1,)), ((), ())), preferred_element_type=F32)


def nn(a, b):
    return jnp.dot(a, b, preferred_element_type=F32)


def tn(a, b):
    return lax.dot_general(a, b, (((0,), (0,)), ((), ())), preferred_element_type=F32)


def copy_of(source, target, sem):
    return pltpu.make_async_copy(source, target, sem)


def head_group(u):
    upper = lax.axis_index("blk") // 8
    return u ^ upper


def pack_kernel(first, heads, with_kv, *refs):
    if with_kv:
        q_ref, do_ref, o_ref, lse_hbm, k_ref, v_ref, msg_ref, buf, o_buf, lse_ref, sem = refs
    else:
        q_ref, do_ref, o_ref, lse_hbm, msg_ref, buf, o_buf, lse_ref, sem = refs
    rows = 2 * heads * TOK + (2 * TOK if with_kv else 0)
    lse_load = copy_of(lse_hbm, lse_ref, sem.at[3, 0])
    lse_load.start()

    groups = [head_group(device_at(i)) for i in range(N_ULY)]
    for u, group in enumerate(groups):

        def load(source, column, at):
            cols = pl.ds(pl.multiple_of(column * D, D), D)
            copy_of(source.at[:, cols], buf.at[u, pl.ds(at, TOK), :], sem.at[0, u]).start()

        o_cols = pl.ds(pl.multiple_of((group * GROUP + first) * D, D), heads * D)
        copy_of(o_ref.at[:, o_cols], o_buf.at[u], sem.at[1, u]).start()
        for j in range(heads):
            load(do_ref, group * GROUP + first + j, (heads + j) * TOK)
        for j in range(heads):
            load(q_ref, group * GROUP + first + j, j * TOK)
        if with_kv:
            load(k_ref, group, 2 * heads * TOK)
            load(v_ref, group, (2 * heads + 1) * TOK)
    row_of = lax.broadcasted_iota(jnp.int32, (8, D), 0)
    lse_load.wait()
    for u in range(N_ULY):
        loaded = buf.at[u, pl.ds(0, rows), :]
        copy_of(loaded, loaded, sem.at[0, u]).wait()
        copy_of(loaded, msg_ref.at[u, pl.ds(0, rows), :], sem.at[2, u]).start()
        copy_of(o_buf.at[u], o_buf.at[u], sem.at[1, u]).wait()
        at = groups[u] * GROUP + first
        stats = jnp.zeros((8, TOK), F32)
        for j in range(heads):
            grads = buf[u, (heads + j) * TOK : (heads + j + 1) * TOK, :].astype(F32)
            product = grads * o_buf[u, :, j * D : (j + 1) * D].astype(F32)
            high = product.astype(BF)
            low = (product - high.astype(F32)).astype(BF)
            ones = jnp.where(row_of == heads + j, 1.0, 0.0).astype(BF)
            stats = stats + nt(ones, high) + nt(ones, low)
            lse_one = lse_ref[pl.ds(at + j, 1), :] * LOG2E
            stats = stats + jnp.where(row_of == j, lse_one, 0.0)
        stats = stats[: 2 * heads]
        p0 = stats.astype(BF).astype(F32)
        p1 = (stats - p0).astype(BF).astype(F32)
        p2 = stats - p0 - p1
        pieces = jnp.concatenate([p0, p1, p2, jnp.zeros_like(p0)], axis=0)
        buf[u, rows : rows + STAT, :] = pieces.astype(BF)
    numbers = pl.ds(rows, STAT)
    last = copy_of(buf.at[:, numbers, :], msg_ref.at[:, numbers, :], sem.at[3, 1])
    last.start()
    for u in range(N_ULY):
        loaded = buf.at[u, pl.ds(0, rows), :]
        copy_of(loaded, msg_ref.at[u, pl.ds(0, rows), :], sem.at[2, u]).wait()
    last.wait()


def pack(queries, grads, outputs, lse, kv, first, heads):
    rows = 2 * heads * TOK + STAT + (2 * TOK if kv else 0)
    message = ((N_ULY, rows, D), BF)
    (msg,) = call(
        functools.partial(pack_kernel, first, heads, bool(kv)),
        [(array, pltpu.HBM) for array in (queries, grads, outputs, lse) + kv],
        ((message, pltpu.HBM),),
        [
            pltpu.VMEM(*message),
            pltpu.VMEM((N_ULY, TOK, heads * D), BF),
            pltpu.VMEM(lse.shape, F32),
            pltpu.SemaphoreType.DMA((4, N_ULY)),
        ],
        1,
        "pack_heads_%d" % first,
    )
    return msg


def slots_of(order_ref):
    slot = lax.axis_index("blk")
    prev = lax.rem(slot + 15, 16)
    a, b = order_ref[0, slot], order_ref[1, slot]
    pa, pb = order_ref[0, prev], order_ref[1, prev]
    low = (a > b).astype(jnp.int32)
    prev_low = (pa > pb).astype(jnp.int32)
    lower_sees = jnp.minimum(a, b) > jnp.minimum(pa, pb)
    return low, prev_low, lower_sees


def half(ref, which, at, odd=None):
    odd = parity() if odd is None else odd
    parts = []
    for b in range(4):
        lower, upper = choose(PLACES, b, odd), choose(PLACES, 4 + b, odd)
        parts.append(ref[lower + which * (upper - lower), at : at + TOK, :])
    return jnp.concatenate(parts, axis=0)


def key_grads(rows, k, v, heads=None):
    q, do, lse, delta = rows
    probs = jnp.exp2(nt(k, q) * (FACTOR * LOG2E) - lse)
    if heads is not None:
        key = lax.broadcasted_iota(jnp.int32, probs.shape, 0)
        row = lax.broadcasted_iota(jnp.int32, probs.shape, 1) % (probs.shape[1] // heads)
        probs = jnp.where(row >= key, probs, 0.0)
    d_scores = (probs * (nt(v, do) - delta) * FACTOR).astype(BF)
    return nn(probs.astype(BF), do), nn(d_scores, q), d_scores


def tile(rows, k, v, heads=None):
    dv, dk, d_scores = key_grads(rows, k, v, heads)
    return dv, dk, tn(d_scores, k)


def stat_rows(x_ref, at):
    parts = []
    for s in range(N_ULY):
        p = x_ref[place_of(s), at : at + STAT, :].astype(F32)
        parts.append(p[0:4] + p[4:8] + p[8:12])
    return jnp.concatenate(parts, axis=1)


def pick(stats, row, which):
    lower, upper = stats[row : row + 1, :HALF], stats[row : row + 1, HALF:]
    return jnp.where(which == 0, lower, upper)


def rows_of(x_ref, stats, heads, which):
    def join(at):
        return jnp.concatenate([half(x_ref, which, (at + j) * TOK) for j in range(heads)], axis=0)

    def join_stats(at):
        return jnp.concatenate([pick(stats, at + j, which) for j in range(heads)], axis=1)

    return join(0), join(heads), join_stats(0), join_stats(heads)


def upper_rows(rows, heads):
    q, do, lse, delta = rows
    q, do = [
        jnp.concatenate([a[j * HALF + 256 : (j + 1) * HALF] for j in range(heads)], 0)
        for a in (q, do)
    ]
    lse, delta = [
        jnp.concatenate([a[:, j * HALF + 256 : (j + 1) * HALF] for j in range(heads)], 1)
        for a in (lse, delta)
    ]
    return q, do, lse, delta


def diagonal(rows, k, v, heads):
    dv0, dk0, dq0 = tile(rows, k[:256], v[:256], heads)
    dv1, dk1, dq1 = tile(upper_rows(rows, heads), k[256:], v[256:], heads)
    dq = []
    for j in range(heads):
        at = j * HALF
        dq.append(dq0[at : at + 256])
        dq.append(dq0[at + 256 : at + HALF] + dq1[j * 256 : (j + 1) * 256])
    return (
        jnp.concatenate([dv0, dv1], 0),
        jnp.concatenate([dk0, dk1], 0),
        jnp.concatenate(dq, 0),
    )


def blocks(value):
    return value.reshape(4, TOK, D)


def put(ref, index, which, value, add=False):
    at = (index, pl.ds(which * 4, 4))
    ref[at] = ref[at] + blocks(value) if add else blocks(value)


def put_heads(ref, heads, which, value, add=False):
    for j in range(heads):
        put(ref, j, which, value[j * HALF : (j + 1) * HALF], add)


def local_tiles(low, x_ref, stats, heads, k_ref, k_at, dq, dkv, after_high):
    high = 1 - low
    k_low, v_low = half(k_ref, low, k_at), half(k_ref, low, k_at + TOK)
    k_high, v_high = half(k_ref, high, k_at), half(k_ref, high, k_at + TOK)
    rows_high = rows_of(x_ref, stats, heads, high)
    rows_low = rows_of(x_ref, stats, heads, low)
    dv2, dk2, dq2 = diagonal(rows_high, k_high, v_high, heads)
    put(dkv, 0, high, dk2)
    put(dkv, 1, high, dv2)
    after_high(high)
    dv, dk, dq1 = tile(rows_high, k_low, v_low)
    put_heads(dq, heads, high, dq1 + dq2)
    dv3, dk3, dq3 = diagonal(rows_low, k_low, v_low, heads)
    put(dkv, 0, low, dk + dk3)
    put(dkv, 1, low, dv + dv3)
    put_heads(dq, heads, low, dq3)


def second_tile(low, prev_low, lower_sees):
    sees = lower_sees.astype(jnp.int32)
    return sees * low + (1 - sees) * (1 - low), sees * prev_low + (1 - sees) * (1 - prev_low)


def cross_tiles(low, prev_low, lower_sees, x_ref, stats, heads, kp_ref, dkv, first, second):
    odd = 1 - parity()

    def one(rows_at, keys_at, take, add):
        k, v = half(kp_ref, keys_at, 0, odd), half(kp_ref, keys_at, TOK, odd)
        dv, dk, d_scores = key_grads(rows_of(x_ref, stats, heads, rows_at), k, v)
        put(dkv, 0, keys_at, dk, add)
        put(dkv, 1, keys_at, dv, add)
        take(rows_at, k, d_scores)

    one(1 - low, prev_low, first, False)
    dkv[:, pl.ds((1 - prev_low) * 4, 4)] = jnp.zeros((2, 4, TOK, D), F32)
    one(*second_tile(low, prev_low, lower_sees), second, True)


def send_rows(out, msg_hbm, at, sem):
    rows = out.shape[1]
    for u in range(N_ULY):
        copy_of(out.at[u], msg_hbm.at[place_of(u), pl.ds(at, rows), :], sem).start()
    return copy_of(out, out, sem)


def local0_kernel(heads, order_ref, x_ref, dq_out, local_hbm, dkv, sem):
    low, _, _ = slots_of(order_ref)
    kv_at = 2 * heads * TOK
    stats = stat_rows(x_ref, kv_at + 2 * TOK)

    def store(which, number):
        part = pl.ds(which * 4, 4)
        return copy_of(dkv.at[:, part], local_hbm.at[:, part], sem.at[number])

    local_tiles(
        low, x_ref, stats, heads, x_ref, kv_at, dq_out, dkv, lambda high: store(high, 1).start()
    )
    store(low, 2).start()
    store(1 - low, 1).wait()
    store(low, 2).wait()


def cross0_kernel(heads, order_ref, x_ref, kp_ref, dq_in, msg_hbm, cross_hbm, dq, dkv, out, sem):
    low, prev_low, lower_sees = slots_of(order_ref)
    stats = stat_rows(x_ref, (2 * heads + 2) * TOK)

    def first(rows_at, k, d_scores):
        put_heads(dq, heads, rows_at, tn(d_scores, k))
        dq[:, pl.ds(low * 4, 4)] = jnp.zeros((heads, 4, TOK, D), F32)

    def second(rows_at, k, d_scores):
        put_heads(dq, heads, rows_at, tn(d_scores, k), True)

    cross_tiles(low, prev_low, lower_sees, x_ref, stats, heads, kp_ref, dkv, first, second)
    store = copy_of(dkv, cross_hbm, sem.at[0])
    store.start()
    for j in range(heads):
        out[:, j * TOK : (j + 1) * TOK, :] = (dq[j] + dq_in[j]).astype(BF)
    send = send_rows(out, msg_hbm, 0, sem.at[1])
    store.wait()
    send.wait()


def cross1_kernel(heads, order_ref, x_ref, kp_ref, cross_hbm, ds_out, cross_out, dkv, held, sem):
    low, prev_low, lower_sees = slots_of(order_ref)
    held_load = copy_of(cross_hbm, held, sem.at[1])
    held_load.start()
    stats = stat_rows(x_ref, 2 * heads * TOK)

    def keep(number):
        def take(rows_at, k, d_scores):
            ds_out[number] = d_scores

        return take

    cross_tiles(low, prev_low, lower_sees, x_ref, stats, heads, kp_ref, dkv, keep(0), keep(1))
    held_load.wait()
    cross_out[...] = (dkv[...] + held[...]).astype(BF)


def local1_kernel(
    heads, kv_at, order_ref, x_ref, x0_ref, kp_ref, ds_ref, local_hbm, msg_in, msg_hbm, local_out,
    dq, held, out, sem,
):
    del msg_in
    low, prev_low, lower_sees = slots_of(order_ref)
    held_load = copy_of(local_hbm, held, sem.at[3])
    held_load.start()
    stats = stat_rows(x_ref, 2 * heads * TOK)
    local_tiles(low, x_ref, stats, heads, x0_ref, kv_at, dq, local_out, lambda high: None)
    odd = 1 - parity()
    tiles = ((1 - low, prev_low), second_tile(low, prev_low, lower_sees))
    for number, (rows_at, keys_at) in enumerate(tiles):
        k = half(kp_ref, keys_at, 0, odd)
        put_heads(dq, heads, rows_at, tn(ds_ref[number], k), True)
    for j in range(heads):
        out[:, j * TOK : (j + 1) * TOK, :] = dq[j].astype(BF)
    send = send_rows(out, msg_hbm, heads * TOK, sem.at[4])
    held_load.wait()
    local_out[...] += held[...]
    send.wait()


def add_kernel(heads, local_ref, back_ref, msg_in, msg_hbm, out, sem):
    del msg_in
    sends = []
    for u in range(N_ULY):
        for i in range(2):
            total = local_ref[i, u] + back_ref[i, u].astype(F32)
            out[u, i * TOK : (i + 1) * TOK, :] = total.astype(BF)
        rows = pl.ds(2 * heads * TOK, 2 * TOK)
        sends.append(copy_of(out.at[u], msg_hbm.at[place_of(u), rows, :], sem.at[u]))
        sends[u].start()
    for send in sends:
        send.wait()


def take_kernel(at, x_ref, out_ref, sem):
    copy = copy_of(x_ref.at[:, pl.ds(at, out_ref.shape[1]), :], out_ref, sem)
    copy.start()
    copy.wait()


def unpack_kernel(x_ref, dq_ref, dk_ref, dv_ref, sem):
    def store(u, at, target, column, which):
        cols = pl.ds(pl.multiple_of(column * D, D), D)
        copy_of(x_ref.at[u, pl.ds(at, TOK), :], target.at[:, cols], sem.at[which]).start()

    for u in range(N_ULY):
        group = head_group(device_at(u))
        for j in range(GROUP):
            store(u, j * TOK, dq_ref, group * GROUP + j, 0)
        store(u, GROUP * TOK, dk_ref, group, 1)
        store(u, (GROUP + 1) * TOK, dv_ref, group, 2)
    for which, ref in enumerate((dq_ref, dk_ref, dv_ref)):
        copy_of(ref, ref, sem.at[which]).wait()


def params():
    return pltpu.CompilerParams(vmem_limit_bytes=32 * MIB)


def shift_slot(value, by):
    pairs = []
    for slot in range(16):
        other = (slot + by) % 16
        flip = 1 if slot // 8 != other // 8 else 0
        pairs += [(slot * N_ULY + u, other * N_ULY + (u ^ flip)) for u in range(N_ULY)]
    return lax.ppermute(value, ("blk", "uly"), pairs)


def exchange(value):
    groups = [[b * N_ULY + u for u in ORDERS[b % 2]] for b in range(16)]
    return lax.all_to_all(
        value, ("blk", "uly"), split_axis=0, concat_axis=0, axis_index_groups=groups, tiled=True
    )


def call(kernel, inputs, outs, scratch, units, name, aliases=None):
    def placed(array, space):
        return pltpu.with_memory_space_constraint(array, space) if space == pltpu.HBM else array

    def shaped(shape, space):
        return pltpu.HBM(*shape) if space == pltpu.HBM else jax.ShapeDtypeStruct(*shape)

    return pl.pallas_call(
        kernel,
        in_specs=[pl.BlockSpec(memory_space=space) for _, space in inputs],
        out_specs=[pl.BlockSpec(memory_space=space) for _, space in outs],
        out_shape=[shaped(shape, space) for shape, space in outs],
        scratch_shapes=scratch,
        input_output_aliases=aliases or {},
        compiler_params=params(),
        cost_estimate=pl.CostEstimate(
            flops=int(units * 5 * 2 * 512 * 512 * 128 * 2),
            bytes_accessed=int(min(units, 4) * MIB),
            transcendentals=int(units * 512 * 512),
        ),
        name=name,
    )(*[placed(array, space) for array, space in inputs])


def body(queries, input_keys, input_values, outputs, output_gradient, saved_logsumexp, span_order):
    h = 2
    kv_at = 2 * h * TOK
    rows4 = (N_ULY, TOK, D)
    lse = saved_logsumexp.T
    order = (span_order.T, pltpu.SMEM)
    msg0 = pack(queries, output_gradient, outputs, lse, (input_keys, input_values), 0, h)
    x0 = exchange(msg0)
    msg1 = pack(queries, output_gradient, outputs, lse, (), h, h)
    x0, msg1 = lax.optimization_barrier((x0, msg1))
    x1 = exchange(msg1)
    (keys,) = call(
        functools.partial(take_kernel, kv_at),
        ((x0, pltpu.VMEM),),
        ((((N_ULY, 2 * TOK, D), BF), pltpu.VMEM),),
        [pltpu.SemaphoreType.DMA],
        0,
        "take_keys",
    )
    kv_prev = shift_slot(keys, 1)

    vmem, hbm = pltpu.VMEM, pltpu.HBM
    head_sums = ((h,) + rows4, F32)
    pair_sums = ((2,) + rows4, F32)
    pair_low = ((2,) + rows4, BF)
    head_low = ((N_ULY, h * TOK, D), BF)
    message = ((N_ULY, (GROUP + 2) * TOK, D), BF)
    sems = pltpu.SemaphoreType.DMA((N_ULY,))
    dq0, local = call(
        functools.partial(local0_kernel, h),
        (order, (x0, vmem)),
        ((head_sums, vmem), (pair_sums, hbm)),
        [pltpu.VMEM(*pair_sums), sems],
        3 * h,
        "local_first",
    )
    msg, cross = call(
        functools.partial(cross0_kernel, h),
        (order, (x0, vmem), (kv_prev, vmem), (dq0, vmem)),
        ((message, hbm), (pair_sums, hbm)),
        [pltpu.VMEM(*head_sums), pltpu.VMEM(*pair_sums), pltpu.VMEM(*head_low), sems],
        2 * h,
        "cross_first",
    )
    d_scores, cross_low = call(
        functools.partial(cross1_kernel, h),
        (order, (x1, vmem), (kv_prev, vmem), (cross, hbm)),
        ((((2, HALF, h * HALF), BF), vmem), (pair_low, vmem)),
        [pltpu.VMEM(*pair_sums), pltpu.VMEM(*pair_sums), sems],
        2 * h,
        "cross_last",
    )
    back = shift_slot(cross_low, -1)
    msg, local = call(
        functools.partial(local1_kernel, h, kv_at),
        (
            order, (x1, vmem), (x0, vmem), (kv_prev, vmem), (d_scores, vmem), (local, hbm),
            (msg, hbm),
        ),
        ((message, hbm), (pair_sums, vmem)),
        [pltpu.VMEM(*head_sums), pltpu.VMEM(*pair_sums), pltpu.VMEM(*head_low), sems],
        3 * h,
        "local_last",
        {6: 0},
    )
    (msg,) = call(
        functools.partial(add_kernel, h),
        ((local, vmem), (back, vmem), (msg, hbm)),
        ((message, hbm),),
        [pltpu.VMEM((N_ULY, 2 * TOK, D), BF), sems],
        0,
        "add_returned",
        {2: 0},
    )
    result = exchange(msg)
    return call(
        unpack_kernel,
        ((result, vmem),),
        (
            (((TOK, N_ULY * GROUP * D), BF), hbm),
            (((TOK, N_ULY * D), BF), hbm),
            (((TOK, N_ULY * D), BF), hbm),
        ),
        [
            pltpu.SemaphoreType.DMA((3,)),
        ],
        0,
        "unpack",
    )


def solution(mesh):
    rows = P(("blk", "uly"), None)
    return jax.shard_map(
        body, mesh=mesh, in_specs=(rows,) * 6 + (P(),), out_specs=(rows,) * 3, check_vma=False
    )
```

```python
import functools
import math

import jax
import jax.numpy as jnp
from jax import lax
from jax.experimental import pallas as pl
from jax.experimental.pallas import tpu as pltpu
from jax.sharding import PartitionSpec as P

D = 128
N_ULY = 8
TOK = 128
GROUP = 4
HALF = 512
FACTOR = 1.0 / math.sqrt(D)
LOG2E = math.log2(math.e)
STAT = 16
BF = jnp.bfloat16
F32 = jnp.float32
MIB = 1 << 20
ORDERS = ((0, 2, 4, 6, 1, 3, 5, 7), (7, 4, 3, 0, 6, 5, 2, 1))
PLACES = tuple(tuple(order.index(u) for u in range(N_ULY)) for order in ORDERS)


def parity():
    return lax.axis_index("blk") % 2


def choose(table, index, odd):
    return table[0][index] + odd * (table[1][index] - table[0][index])


def device_at(place):
    return choose(ORDERS, place, parity())


def place_of(u):
    return choose(PLACES, u, parity())


def nt(a, b):
    return lax.dot_general(a, b, (((1,), (1,)), ((), ())), preferred_element_type=F32)


def nn(a, b):
    return jnp.dot(a, b, preferred_element_type=F32)


def tn(a, b):
    return lax.dot_general(a, b, (((0,), (0,)), ((), ())), preferred_element_type=F32)


def copy_of(source, target, sem):
    return pltpu.make_async_copy(source, target, sem)


def head_group(u):
    upper = lax.axis_index("blk") // 8
    return u ^ upper


def pack_kernel(first, heads, with_kv, *refs):
    if with_kv:
        q_ref, do_ref, o_ref, lse_hbm, k_ref, v_ref, msg_ref, buf, o_buf, lse_ref, sem = refs
    else:
        q_ref, do_ref, o_ref, lse_hbm, msg_ref, buf, o_buf, lse_ref, sem = refs
    rows = 2 * heads * TOK + (2 * TOK if with_kv else 0)
    lse_load = copy_of(lse_hbm, lse_ref, sem.at[3, 0])
    lse_load.start()

    groups = [head_group(device_at(i)) for i in range(N_ULY)]
    for u, group in enumerate(groups):

        def load(source, column, at):
            cols = pl.ds(pl.multiple_of(column * D, D), D)
            copy_of(source.at[:, cols], buf.at[u, pl.ds(at, TOK), :], sem.at[0, u]).start()

        o_cols = pl.ds(pl.multiple_of((group * GROUP + first) * D, D), heads * D)
        copy_of(o_ref.at[:, o_cols], o_buf.at[u], sem.at[1, u]).start()
        for j in range(heads):
            load(do_ref, group * GROUP + first + j, (heads + j) * TOK)
        for j in range(heads):
            load(q_ref, group * GROUP + first + j, j * TOK)
        if with_kv:
            load(k_ref, group, 2 * heads * TOK)
            load(v_ref, group, (2 * heads + 1) * TOK)
    row_of = lax.broadcasted_iota(jnp.int32, (8, D), 0)
    lse_load.wait()
    for u in range(N_ULY):
        loaded = buf.at[u, pl.ds(0, rows), :]
        copy_of(loaded, loaded, sem.at[0, u]).wait()
        copy_of(loaded, msg_ref.at[u, pl.ds(0, rows), :], sem.at[2, u]).start()
        copy_of(o_buf.at[u], o_buf.at[u], sem.at[1, u]).wait()
        at = groups[u] * GROUP + first
        stats = jnp.zeros((8, TOK), F32)
        for j in range(heads):
            grads = buf[u, (heads + j) * TOK : (heads + j + 1) * TOK, :].astype(F32)
            product = grads * o_buf[u, :, j * D : (j + 1) * D].astype(F32)
            high = product.astype(BF)
            low = (product - high.astype(F32)).astype(BF)
            ones = jnp.where(row_of == heads + j, 1.0, 0.0).astype(BF)
            stats = stats + nt(ones, high) + nt(ones, low)
            lse_one = lse_ref[pl.ds(at + j, 1), :] * LOG2E
            stats = stats + jnp.where(row_of == j, lse_one, 0.0)
        stats = stats[: 2 * heads]
        p0 = stats.astype(BF).astype(F32)
        p1 = (stats - p0).astype(BF).astype(F32)
        p2 = stats - p0 - p1
        pieces = jnp.concatenate([p0, p1, p2, jnp.zeros_like(p0)], axis=0)
        buf[u, rows : rows + STAT, :] = pieces.astype(BF)
    numbers = pl.ds(rows, STAT)
    last = copy_of(buf.at[:, numbers, :], msg_ref.at[:, numbers, :], sem.at[3, 1])
    last.start()
    for u in range(N_ULY):
        loaded = buf.at[u, pl.ds(0, rows), :]
        copy_of(loaded, msg_ref.at[u, pl.ds(0, rows), :], sem.at[2, u]).wait()
    last.wait()


def pack(queries, grads, outputs, lse, kv, first, heads):
    rows = 2 * heads * TOK + STAT + (2 * TOK if kv else 0)
    message = ((N_ULY, rows, D), BF)
    (msg,) = call(
        functools.partial(pack_kernel, first, heads, bool(kv)),
        [(array, pltpu.HBM) for array in (queries, grads, outputs, lse) + kv],
        ((message, pltpu.HBM),),
        [
            pltpu.VMEM(*message),
            pltpu.VMEM((N_ULY, TOK, heads * D), BF),
            pltpu.VMEM(lse.shape, F32),
            pltpu.SemaphoreType.DMA((4, N_ULY)),
        ],
        1,
        "pack_heads_%d" % first,
    )
    return msg


def slots_of(order_ref):
    slot = lax.axis_index("blk")
    prev = lax.rem(slot + 15, 16)
    a, b = order_ref[0, slot], order_ref[1, slot]
    pa, pb = order_ref[0, prev], order_ref[1, prev]
    low = (a > b).astype(jnp.int32)
    prev_low = (pa > pb).astype(jnp.int32)
    lower_sees = jnp.minimum(a, b) > jnp.minimum(pa, pb)
    return low, prev_low, lower_sees


def half(ref, which, at, odd=None):
    odd = parity() if odd is None else odd
    parts = []
    for b in range(4):
        lower, upper = choose(PLACES, b, odd), choose(PLACES, 4 + b, odd)
        parts.append(ref[lower + which * (upper - lower), at : at + TOK, :])
    return jnp.concatenate(parts, axis=0)


def key_grads(rows, k, v, heads=None):
    q, do, lse, delta = rows
    probs = jnp.exp2(nt(k, q) * (FACTOR * LOG2E) - lse)
    if heads is not None:
        key = lax.broadcasted_iota(jnp.int32, probs.shape, 0)
        row = lax.broadcasted_iota(jnp.int32, probs.shape, 1) % (probs.shape[1] // heads)
        probs = jnp.where(row >= key, probs, 0.0)
    d_scores = (probs * (nt(v, do) - delta) * FACTOR).astype(BF)
    return nn(probs.astype(BF), do), nn(d_scores, q), d_scores


def tile(rows, k, v, heads=None):
    dv, dk, d_scores = key_grads(rows, k, v, heads)
    return dv, dk, tn(d_scores, k)


def stat_rows(x_ref, at):
    parts = []
    for s in range(N_ULY):
        p = x_ref[place_of(s), at : at + STAT, :].astype(F32)
        parts.append(p[0:4] + p[4:8] + p[8:12])
    return jnp.concatenate(parts, axis=1)


def pick(stats, row, which):
    lower, upper = stats[row : row + 1, :HALF], stats[row : row + 1, HALF:]
    return jnp.where(which == 0, lower, upper)


def rows_of(x_ref, stats, heads, which):
    def join(at):
        return jnp.concatenate([half(x_ref, which, (at + j) * TOK) for j in range(heads)], axis=0)

    def join_stats(at):
        return jnp.concatenate([pick(stats, at + j, which) for j in range(heads)], axis=1)

    return join(0), join(heads), join_stats(0), join_stats(heads)


def upper_rows(rows, heads):
    q, do, lse, delta = rows
    q, do = [
        jnp.concatenate([a[j * HALF + 256 : (j + 1) * HALF] for j in range(heads)], 0)
        for a in (q, do)
    ]
    lse, delta = [
        jnp.concatenate([a[:, j * HALF + 256 : (j + 1) * HALF] for j in range(heads)], 1)
        for a in (lse, delta)
    ]
    return q, do, lse, delta


def diagonal(rows, k, v, heads):
    dv0, dk0, dq0 = tile(rows, k[:256], v[:256], heads)
    dv1, dk1, dq1 = tile(upper_rows(rows, heads), k[256:], v[256:], heads)
    dq = []
    for j in range(heads):
        at = j * HALF
        dq.append(dq0[at : at + 256])
        dq.append(dq0[at + 256 : at + HALF] + dq1[j * 256 : (j + 1) * 256])
    return (
        jnp.concatenate([dv0, dv1], 0),
        jnp.concatenate([dk0, dk1], 0),
        jnp.concatenate(dq, 0),
    )


def blocks(value):
    return value.reshape(4, TOK, D)


def put(ref, index, which, value, add=False):
    at = (index, pl.ds(which * 4, 4))
    ref[at] = ref[at] + blocks(value) if add else blocks(value)


def put_heads(ref, heads, which, value, add=False):
    for j in range(heads):
        put(ref, j, which, value[j * HALF : (j + 1) * HALF], add)


def local_tiles(low, x_ref, stats, heads, k_ref, k_at, dq, dkv, after_high):
    high = 1 - low
    k_low, v_low = half(k_ref, low, k_at), half(k_ref, low, k_at + TOK)
    k_high, v_high = half(k_ref, high, k_at), half(k_ref, high, k_at + TOK)
    rows_high = rows_of(x_ref, stats, heads, high)
    rows_low = rows_of(x_ref, stats, heads, low)
    dv2, dk2, dq2 = diagonal(rows_high, k_high, v_high, heads)
    put(dkv, 0, high, dk2)
    put(dkv, 1, high, dv2)
    after_high(high)
    dv, dk, dq1 = tile(rows_high, k_low, v_low)
    put_heads(dq, heads, high, dq1 + dq2)
    dv3, dk3, dq3 = diagonal(rows_low, k_low, v_low, heads)
    put(dkv, 0, low, dk + dk3)
    put(dkv, 1, low, dv + dv3)
    put_heads(dq, heads, low, dq3)


def second_tile(low, prev_low, lower_sees):
    sees = lower_sees.astype(jnp.int32)
    return sees * low + (1 - sees) * (1 - low), sees * prev_low + (1 - sees) * (1 - prev_low)


def cross_tiles(low, prev_low, lower_sees, x_ref, stats, heads, kp_ref, dkv, first, second):
    odd = 1 - parity()

    def one(rows_at, keys_at, take, add):
        k, v = half(kp_ref, keys_at, 0, odd), half(kp_ref, keys_at, TOK, odd)
        dv, dk, d_scores = key_grads(rows_of(x_ref, stats, heads, rows_at), k, v)
        put(dkv, 0, keys_at, dk, add)
        put(dkv, 1, keys_at, dv, add)
        take(rows_at, k, d_scores)

    one(1 - low, prev_low, first, False)
    dkv[:, pl.ds((1 - prev_low) * 4, 4)] = jnp.zeros((2, 4, TOK, D), F32)
    one(*second_tile(low, prev_low, lower_sees), second, True)


def send_rows(out, msg_hbm, at, sem):
    rows = out.shape[1]
    for u in range(N_ULY):
        copy_of(out.at[u], msg_hbm.at[place_of(u), pl.ds(at, rows), :], sem).start()
    return copy_of(out, out, sem)


def local0_kernel(heads, order_ref, x_ref, dq_out, local_hbm, dkv, sem):
    low, _, _ = slots_of(order_ref)
    kv_at = 2 * heads * TOK
    stats = stat_rows(x_ref, kv_at + 2 * TOK)

    def store(which, number):
        part = pl.ds(which * 4, 4)
        return copy_of(dkv.at[:, part], local_hbm.at[:, part], sem.at[number])

    local_tiles(
        low, x_ref, stats, heads, x_ref, kv_at, dq_out, dkv, lambda high: store(high, 1).start()
    )
    store(low, 2).start()
    store(1 - low, 1).wait()
    store(low, 2).wait()


def cross0_kernel(heads, order_ref, x_ref, kp_ref, dq_in, msg_hbm, cross_hbm, dq, dkv, out, sem):
    low, prev_low, lower_sees = slots_of(order_ref)
    stats = stat_rows(x_ref, (2 * heads + 2) * TOK)

    def first(rows_at, k, d_scores):
        put_heads(dq, heads, rows_at, tn(d_scores, k))
        dq[:, pl.ds(low * 4, 4)] = jnp.zeros((heads, 4, TOK, D), F32)

    def second(rows_at, k, d_scores):
        put_heads(dq, heads, rows_at, tn(d_scores, k), True)

    cross_tiles(low, prev_low, lower_sees, x_ref, stats, heads, kp_ref, dkv, first, second)
    store = copy_of(dkv, cross_hbm, sem.at[0])
    store.start()
    sends = []
    for j in range(heads):
        rows = pl.ds(j * TOK, TOK)
        out[:, j * TOK : (j + 1) * TOK, :] = (dq[j] + dq_in[j]).astype(BF)
        for u in range(N_ULY):
            target = msg_hbm.at[place_of(u), rows, :]
            copy_of(out.at[u, rows, :], target, sem.at[1 + j]).start()
        sends.append(copy_of(out.at[:, rows, :], out.at[:, rows, :], sem.at[1 + j]))
    store.wait()
    for send in sends:
        send.wait()


def cross1_kernel(heads, order_ref, x_ref, kp_ref, cross_hbm, ds_out, cross_out, dkv, held, sem):
    low, prev_low, lower_sees = slots_of(order_ref)
    held_load = copy_of(cross_hbm, held, sem.at[1])
    held_load.start()
    stats = stat_rows(x_ref, 2 * heads * TOK)

    def keep(number):
        def take(rows_at, k, d_scores):
            ds_out[number] = d_scores

        return take

    cross_tiles(low, prev_low, lower_sees, x_ref, stats, heads, kp_ref, dkv, keep(0), keep(1))
    held_load.wait()
    cross_out[...] = (dkv[...] + held[...]).astype(BF)


def local1_kernel(
    heads, kv_at, order_ref, x_ref, x0_ref, kp_ref, ds_ref, local_hbm, msg_in, msg_hbm, local_out,
    dq, held, out, sem,
):
    del msg_in
    low, prev_low, lower_sees = slots_of(order_ref)
    held_load = copy_of(local_hbm, held, sem.at[3])
    held_load.start()
    stats = stat_rows(x_ref, 2 * heads * TOK)
    local_tiles(low, x_ref, stats, heads, x0_ref, kv_at, dq, local_out, lambda high: None)
    odd = 1 - parity()
    tiles = ((1 - low, prev_low), second_tile(low, prev_low, lower_sees))
    for number, (rows_at, keys_at) in enumerate(tiles):
        k = half(kp_ref, keys_at, 0, odd)
        put_heads(dq, heads, rows_at, tn(ds_ref[number], k), True)
    for j in range(heads):
        out[:, j * TOK : (j + 1) * TOK, :] = dq[j].astype(BF)
    send = send_rows(out, msg_hbm, heads * TOK, sem.at[4])
    held_load.wait()
    local_out[...] += held[...]
    send.wait()


def add_kernel(heads, local_ref, back_ref, msg_in, msg_hbm, out, sem):
    del msg_in
    sends = []
    for u in range(N_ULY):
        for i in range(2):
            total = local_ref[i, u] + back_ref[i, u].astype(F32)
            out[u, i * TOK : (i + 1) * TOK, :] = total.astype(BF)
        rows = pl.ds(2 * heads * TOK, 2 * TOK)
        sends.append(copy_of(out.at[u], msg_hbm.at[place_of(u), rows, :], sem.at[u]))
        sends[u].start()
    for send in sends:
        send.wait()


def take_kernel(at, x_ref, out_ref, sem):
    copy = copy_of(x_ref.at[:, pl.ds(at, out_ref.shape[1]), :], out_ref, sem)
    copy.start()
    copy.wait()


def unpack_kernel(x_ref, dq_ref, dk_ref, dv_ref, sem):
    def store(u, at, target, column, which):
        cols = pl.ds(pl.multiple_of(column * D, D), D)
        copy_of(x_ref.at[u, pl.ds(at, TOK), :], target.at[:, cols], sem.at[which]).start()

    for u in range(N_ULY):
        group = head_group(device_at(u))
        for j in range(GROUP):
            store(u, j * TOK, dq_ref, group * GROUP + j, 0)
        store(u, GROUP * TOK, dk_ref, group, 1)
        store(u, (GROUP + 1) * TOK, dv_ref, group, 2)
    for which, ref in enumerate((dq_ref, dk_ref, dv_ref)):
        copy_of(ref, ref, sem.at[which]).wait()


def params():
    return pltpu.CompilerParams(vmem_limit_bytes=32 * MIB)


def shift_slot(value, by):
    pairs = []
    for slot in range(16):
        other = (slot + by) % 16
        flip = 1 if slot // 8 != other // 8 else 0
        pairs += [(slot * N_ULY + u, other * N_ULY + (u ^ flip)) for u in range(N_ULY)]
    return lax.ppermute(value, ("blk", "uly"), pairs)


def exchange(value):
    groups = [[b * N_ULY + u for u in ORDERS[b % 2]] for b in range(16)]
    return lax.all_to_all(
        value, ("blk", "uly"), split_axis=0, concat_axis=0, axis_index_groups=groups, tiled=True
    )


def call(kernel, inputs, outs, scratch, units, name, aliases=None):
    def placed(array, space):
        return pltpu.with_memory_space_constraint(array, space) if space == pltpu.HBM else array

    def shaped(shape, space):
        return pltpu.HBM(*shape) if space == pltpu.HBM else jax.ShapeDtypeStruct(*shape)

    return pl.pallas_call(
        kernel,
        in_specs=[pl.BlockSpec(memory_space=space) for _, space in inputs],
        out_specs=[pl.BlockSpec(memory_space=space) for _, space in outs],
        out_shape=[shaped(shape, space) for shape, space in outs],
        scratch_shapes=scratch,
        input_output_aliases=aliases or {},
        compiler_params=params(),
        cost_estimate=pl.CostEstimate(
            flops=int(units * 5 * 2 * 512 * 512 * 128 * 2),
            bytes_accessed=int(min(units, 4) * MIB),
            transcendentals=int(units * 512 * 512),
        ),
        name=name,
    )(*[placed(array, space) for array, space in inputs])


def body(queries, input_keys, input_values, outputs, output_gradient, saved_logsumexp, span_order):
    h = 2
    kv_at = 2 * h * TOK
    rows4 = (N_ULY, TOK, D)
    lse = saved_logsumexp.T
    order = (span_order.T, pltpu.SMEM)
    msg0 = pack(queries, output_gradient, outputs, lse, (input_keys, input_values), 0, h)
    x0 = exchange(msg0)
    msg1 = pack(queries, output_gradient, outputs, lse, (), h, h)
    x0, msg1 = lax.optimization_barrier((x0, msg1))
    x1 = exchange(msg1)
    (keys,) = call(
        functools.partial(take_kernel, kv_at),
        ((x0, pltpu.VMEM),),
        ((((N_ULY, 2 * TOK, D), BF), pltpu.VMEM),),
        [pltpu.SemaphoreType.DMA],
        0,
        "take_keys",
    )
    kv_prev = shift_slot(keys, 1)

    vmem, hbm = pltpu.VMEM, pltpu.HBM
    head_sums = ((h,) + rows4, F32)
    pair_sums = ((2,) + rows4, F32)
    pair_low = ((2,) + rows4, BF)
    head_low = ((N_ULY, h * TOK, D), BF)
    message = ((N_ULY, (GROUP + 2) * TOK, D), BF)
    sems = pltpu.SemaphoreType.DMA((N_ULY,))
    dq0, local = call(
        functools.partial(local0_kernel, h),
        (order, (x0, vmem)),
        ((head_sums, vmem), (pair_sums, hbm)),
        [pltpu.VMEM(*pair_sums), sems],
        3 * h,
        "local_first",
    )
    msg, cross = call(
        functools.partial(cross0_kernel, h),
        (order, (x0, vmem), (kv_prev, vmem), (dq0, vmem)),
        ((message, hbm), (pair_sums, hbm)),
        [pltpu.VMEM(*head_sums), pltpu.VMEM(*pair_sums), pltpu.VMEM(*head_low), sems],
        2 * h,
        "cross_first",
    )
    d_scores, cross_low = call(
        functools.partial(cross1_kernel, h),
        (order, (x1, vmem), (kv_prev, vmem), (cross, hbm)),
        ((((2, HALF, h * HALF), BF), vmem), (pair_low, vmem)),
        [pltpu.VMEM(*pair_sums), pltpu.VMEM(*pair_sums), sems],
        2 * h,
        "cross_last",
    )
    back = shift_slot(cross_low, -1)
    msg, local = call(
        functools.partial(local1_kernel, h, kv_at),
        (
            order, (x1, vmem), (x0, vmem), (kv_prev, vmem), (d_scores, vmem), (local, hbm),
            (msg, hbm),
        ),
        ((message, hbm), (pair_sums, vmem)),
        [pltpu.VMEM(*head_sums), pltpu.VMEM(*pair_sums), pltpu.VMEM(*head_low), sems],
        3 * h,
        "local_last",
        {6: 0},
    )
    (msg,) = call(
        functools.partial(add_kernel, h),
        ((local, vmem), (back, vmem), (msg, hbm)),
        ((message, hbm),),
        [pltpu.VMEM((N_ULY, 2 * TOK, D), BF), sems],
        0,
        "add_returned",
        {2: 0},
    )
    result = exchange(msg)
    return call(
        unpack_kernel,
        ((result, vmem),),
        (
            (((TOK, N_ULY * GROUP * D), BF), hbm),
            (((TOK, N_ULY * D), BF), hbm),
            (((TOK, N_ULY * D), BF), hbm),
        ),
        [
            pltpu.SemaphoreType.DMA((3,)),
        ],
        0,
        "unpack",
    )


def solution(mesh):
    rows = P(("blk", "uly"), None)
    return jax.shard_map(
        body, mesh=mesh, in_specs=(rows,) * 6 + (P(),), out_specs=(rows,) * 3, check_vma=False
    )
```
